512 devices in a mesh: shell: 8 (over y), lat: 64 (over x, z, core).
Axes of the slice: x: 4, y: 8, z: 8, core: 2. Of those that a mesh axis runs over, the one named last changes fastest.
Arguments:
- solution: float32 [3, 64, 4096, 128], P(None, 'shell', 'lat'), may hold values from -6 to 6
- right_side: float32 [3, 64, 4096, 128], P(None, 'shell', 'lat'), may hold values from -20000 to 20000
- viscosity: float32 [64, 4096, 128], P('shell', 'lat'), may hold values from 3e-05 to 30000, as said below
- stencil_weights: float32 [7], replicated, may hold values from 0.3 to 3
Outputs:
- smoothed: float32 [3, 64, 4096, 128], P(None, 'shell', 'lat')
- coarse: float32 [3, 32, 2048, 64], P(None, 'shell', 'lat')
The draws below stay inside these ranges and needn't reach their ends.
Inputs may be any that keep to these rules, and one draw needn't show every extreme that they name: `viscosity`: positive.
All inputs are finite; a program needn't handle non-finite values.
Results may differ from the reference program's by a relative error of at most 0.00002.
Values sent between devices are 32-bit elements; how exact they have to be, the bound alone decides.
No kernel may reach another device: no remote copies, remote signals or barrier semaphores. Data moves between devices by JAX's collectives and lax.ppermute only.
A program may use at most 64 MiB of HBM per device.

```python
import math
import jax
import jax.numpy as jnp
from jax import lax

COMP = 3
CB = 128
NR = 64
NA = 4096


def layer_profile():
    radial = jnp.arange(NR, dtype=jnp.float32) / (NR - 1)
    return (-3.0 + 6.0 * radial)[:, None, None]


def draw_viscosity(key, part):
    key = jax.random.fold_in(key, 11)
    rough = jax.random.uniform(key, (NR, NA, CB), jnp.float32, -0.45, 0.45)
    power = layer_profile() + rough
    return jnp.power(10.0, power).astype(jnp.float32)


def draw_right_side(key, part):
    key = jax.random.fold_in(key, 23)
    scale = 3.0 * jnp.power(10.0, layer_profile())[None]
    values = jnp.clip(jax.random.normal(key, (COMP, NR, NA, CB), jnp.float32), -4.0, 4.0)
    return (scale * values).astype(jnp.float32)


def level_of(rng, dims, shards, low, top_value):
    def one(axis_at, blocks):
        steps = jax.random.uniform(jax.random.fold_in(jax.random.fold_in(rng, 6), axis_at), (blocks,), jnp.float32, low / len(shards), top_value / len(shards))
        return jnp.repeat(jnp.exp(steps), dims[axis_at] // blocks).reshape((-1,) + (1,) * (len(dims) - axis_at - 1))

    factor_of = one(*shards[0])
    for cut in shards[1:]:
        factor_of = factor_of * one(*cut)
    return factor_of


def centred(stream_key, extent, spread, limit, cuts=(), kind=jnp.bfloat16):
    values = spread * jax.random.normal(stream_key, extent, jnp.float32)
    if cuts:
        values = values * level_of(stream_key, extent, cuts, -0.22, 0.18)
    return jnp.clip(values, -limit, limit).astype(kind)


def setup_inputs(seed: int = 0) -> dict:
    seeds = jax.random.split(jax.random.key(seed), 5)
    solution = centred(seeds[0], (COMP, NR, NA, CB), 1.0, 6.0, ((1, 8), (2, 64)), jnp.float32)
    right_side = draw_right_side(jax.random.fold_in(seeds[4], 71), 0)
    viscosity = draw_viscosity(jax.random.fold_in(seeds[4], 71), 0)
    stencil_weights = jnp.clip(jnp.exp(jax.random.uniform(seeds[3], (7,), jnp.float32, math.log(0.3), math.log(3.0))), 0.3, 3.0)
    return dict(solution=solution, right_side=right_side, viscosity=viscosity, stencil_weights=stencil_weights)


OFFSETS = ((1, 0, 0), (0, 1, 0), (0, 0, 1), (1, 1, 0), (1, 0, 1), (0, 1, 1), (1, 1, 1))
OMEGA = 0.6


def moved(field, first, second, third):
    size_a, size_b, size_c = field.shape[-3:]
    return field[..., 1 + first:size_a - 1 + first, 1 + second:size_b - 1 + second, 1 + third:size_c - 1 + third]


def stencil(upad, npad, weights):
    uz = jnp.pad(upad, ((0, 0), (0, 0), (0, 0), (1, 1)))
    nz = jnp.pad(npad, ((0, 0), (0, 0), (1, 1)))
    ucenter = moved(uz, 0, 0, 0)
    ncenter = moved(nz, 0, 0, 0)
    diag = jnp.zeros_like(ncenter)
    offsum = jnp.zeros_like(ucenter)
    for index, step in enumerate(OFFSETS):
        for sign in (1, -1):
            coef = weights[index] * 0.5 * (ncenter + moved(nz, sign * step[0], sign * step[1], sign * step[2]))
            diag = diag + coef
            offsum = offsum + coef * moved(uz, sign * step[0], sign * step[1], sign * step[2])
    return diag * ucenter - offsum, diag, ucenter


def halve(field, axis, following):
    count = field.shape[axis]
    joined = jnp.concatenate([field, following], axis)
    first = lax.slice_in_dim(joined, 0, count, 2, axis)
    middle = lax.slice_in_dim(joined, 1, count, 2, axis)
    last = lax.slice_in_dim(joined, 2, count + 1, 2, axis)
    return 0.25 * first + 0.5 * middle + 0.25 * last


def restrict_all(scaled, upper, beside):
    radial = halve(scaled, 1, upper)
    lateral = halve(radial, 2, beside(radial))
    tail = jnp.zeros_like(lateral[:, :, :, 0:1])
    return halve(lateral, 3, tail)


def reference(solution, right_side, viscosity, stencil_weights):
    npad = jnp.pad(viscosity, ((1, 1), (1, 1), (0, 0)))
    current = solution
    for turn in range(3):
        upad = jnp.pad(current, ((0, 0), (1, 1), (1, 1), (0, 0)))
        image, diag, ucenter = stencil(upad, npad, stencil_weights)
        if turn < 2:
            current = current + OMEGA * (right_side - image) / diag
    scaled = (right_side - image) / diag
    upper = jnp.zeros_like(scaled[:, 0:1])

    def beside(radial):
        return jnp.zeros_like(radial[:, :, 0:1])

    return current, restrict_all(scaled, upper, beside)
```

```python
import jax
import jax.numpy as jnp
from jax import lax
from jax.experimental import pallas as pl
from jax.experimental.pallas import tpu as pltpu
from jax.sharding import PartitionSpec as P

OMEGA = 0.6
COMP = 3
BELOW = 3
ABOVE = 4
TILE = 8


def pack_kernel(u, rhs, visc, to_below, to_above, to_left, to_right, sems):
    rows, cols = visc.shape[0], visc.shape[1]
    copies = []

    def copy(src, dst):
        copies.append(pltpu.make_async_copy(src, dst, sems.at[len(copies)]))
        copies[-1].start()

    def rows_of(buffer, count, first_n, first_r, count_r):
        at = 0
        for c in range(COMP):
            copy(u.at[c, pl.ds(first_n, count)], buffer.at[pl.ds(at, count)])
            at += count
        copy(visc.at[pl.ds(first_n, count)], buffer.at[pl.ds(at, count)])
        at += count
        for c in range(COMP):
            copy(rhs.at[c, pl.ds(first_r, count_r)], buffer.at[pl.ds(at, count_r)])
            at += count_r

    rows_of(to_below, ABOVE, 0, 0, ABOVE - 1)
    rows_of(to_above, BELOW, rows - BELOW, rows - BELOW + 1, BELOW - 1)
    for buffer, first in ((to_left, 0), (to_right, cols - TILE)):
        copy(u.at[:, :, pl.ds(first, TILE)], buffer.at[pl.ds(0, COMP)])
        copy(rhs.at[:, :, pl.ds(first, TILE)], buffer.at[pl.ds(COMP, COMP)])
        copy(visc.at[:, pl.ds(first, TILE)], buffer.at[2 * COMP])
    for each in copies:
        each.wait()


def pack(u, rhs, visc):
    rows, cols, lanes = visc.shape
    f32 = jnp.float32
    shapes = (
        ((4 * ABOVE + 3 * (ABOVE - 1)), cols, lanes),
        ((4 * BELOW + 3 * (BELOW - 1)), cols, lanes),
        (2 * COMP + 1, rows, TILE, lanes),
        (2 * COMP + 1, rows, TILE, lanes),
    )
    return pl.pallas_call(
        pack_kernel,
        out_shape=[jax.ShapeDtypeStruct(s, f32) for s in shapes],
        in_specs=[pl.BlockSpec(memory_space=pl.ANY)] * 3,
        out_specs=[pl.BlockSpec(memory_space=pltpu.VMEM)] * 4,
        scratch_shapes=[pltpu.SemaphoreType.DMA((20,))],
        compiler_params=pltpu.CompilerParams(vmem_limit_bytes=8 << 20),
        cost_estimate=pl.CostEstimate(flops=0, bytes_accessed=4 << 20, transcendentals=0),
        name="pack",
    )(u, rhs, visc)


def corner_kernel(left, right, to_below, to_above):
    rows = left.shape[1]
    late = lax.broadcasted_iota(jnp.int32, left.shape[2:], 0) >= TILE - BELOW

    def rows_of(buffer, count, first_n, first_r, count_r):
        at = 0
        picks = [(c, first_n + i) for c in range(COMP) for i in range(count)]
        picks += [(2 * COMP, first_n + i) for i in range(count)]
        picks += [(COMP + c, first_r + i) for c in range(COMP) for i in range(count_r)]
        for field, row in picks:
            buffer[at] = jnp.where(late, left[field, row], right[field, row])
            at += 1

    rows_of(to_below, ABOVE, 0, 0, ABOVE - 1)
    rows_of(to_above, BELOW, rows - BELOW, rows - BELOW + 1, BELOW - 1)


def corners(left, right):
    lanes = left.shape[-1]
    shapes = (
        ((4 * ABOVE + 3 * (ABOVE - 1)), TILE, lanes),
        ((4 * BELOW + 3 * (BELOW - 1)), TILE, lanes),
    )
    return pl.pallas_call(
        corner_kernel,
        out_shape=[jax.ShapeDtypeStruct(s, jnp.float32) for s in shapes],
        in_specs=[pl.BlockSpec(memory_space=pltpu.VMEM)] * 2,
        out_specs=[pl.BlockSpec(memory_space=pltpu.VMEM)] * 2,
        compiler_params=pltpu.CompilerParams(vmem_limit_bytes=8 << 20),
        cost_estimate=pl.CostEstimate(flops=0, bytes_accessed=1 << 20, transcendentals=0),
        name="corners",
    )(left, right)


def smooth_kernel(
    wts, u, rhs, visc, left, right, above, below, above_c, below_c,
    smoothed, coarse,
    u0, u1, u2, force, n, coef, inv, carry, moved, restr,
):
    rows, cols, lanes = visc.shape
    wide = cols + TILE
    sub = lax.broadcasted_iota(jnp.int32, (TILE, lanes), 0)
    late = sub >= TILE - BELOW
    own = slice(BELOW, BELOW + rows)
    main, side = slice(0, cols), slice(cols, wide)

    for c in range(COMP):
        u0[c, own, main] = u[c]
        force[c, own, main] = rhs[c]
        u0[c, own, side] = jnp.where(late, left[c], right[c])
        force[c, own, side] = jnp.where(late, left[COMP + c], right[COMP + c])
        a, b = ABOVE * c, BELOW * c
        u0[c, BELOW + rows :, main] = above[a : a + ABOVE]
        u0[c, BELOW + rows :, side] = above_c[a : a + ABOVE]
        u0[c, 0:BELOW, main] = below[b : b + BELOW]
        u0[c, 0:BELOW, side] = below_c[b : b + BELOW]
        a, b = 4 * ABOVE + (ABOVE - 1) * c, 4 * BELOW + (BELOW - 1) * c
        force[c, BELOW + rows : BELOW + rows + ABOVE - 1, main] = above[a : a + ABOVE - 1]
        force[c, BELOW + rows : BELOW + rows + ABOVE - 1, side] = above_c[a : a + ABOVE - 1]
        force[c, 1:BELOW, main] = below[b : b + BELOW - 1]
        force[c, 1:BELOW, side] = below_c[b : b + BELOW - 1]
    n[own, main] = visc[...]
    n[own, side] = jnp.where(late, left[2 * COMP], right[2 * COMP])
    n[BELOW + rows :, main] = above[3 * ABOVE : 4 * ABOVE]
    n[BELOW + rows :, side] = above_c[3 * ABOVE : 4 * ABOVE]
    n[0:BELOW, main] = below[3 * BELOW : 4 * BELOW]
    n[0:BELOW, side] = below_c[3 * BELOW : 4 * BELOW]

    def sl(x):
        return pltpu.roll(x, wide - 1, 0)

    def sl_back(x):
        return pltpu.roll(x, 1, 0)

    def sc(x):
        return pltpu.roll(x, lanes - 1, 1)

    def sc_back(x):
        return pltpu.roll(x, 1, 1)

    lane = lax.broadcasted_iota(jnp.int32, (1, lanes), 1)
    half = [0.5 * wts[k] for k in range(7)]
    w = [
        jnp.where(lane < lanes - 1, half[k], 0.0) if k in (2, 4, 5, 6) else half[k]
        for k in range(7)
    ]
    lost = half[2] + half[4] + half[5] + half[6]
    rim = jnp.where((lane == 0) | (lane == lanes - 1), lost, 0.0)

    def edges(at, move):
        low, high = n[at], n[at + 1]
        low_l, high_l = sl(low), sl(high)
        coef[0, at] = w[0] * (low + high)
        coef[1, at] = w[1] * (low + low_l)
        coef[2, at] = w[2] * (low + sc(low))
        coef[3, at] = w[3] * (low + high_l)
        coef[4, at] = w[4] * (low + sc(high))
        coef[5, at] = w[5] * (low + sc(low_l))
        coef[6, at] = w[6] * (low + sc(high_l))

    last = BELOW + rows + ABOVE - 1

    def edges_step(at, _):
        edges(at, None)
        return 0

    lax.fori_loop(0, last, edges_step, 0)

    def diag_step(at, _):
        e = [coef[k, at] for k in range(7)]
        p = {k: coef[k, at - 1] for k in (0, 3, 4, 6)}
        low = n[at]
        total = e[0] + e[1] + e[2] + e[3] + e[4] + e[5] + e[6] + p[0] + rim * low
        total = total + sc_back(e[2] + p[4]) + sl_back(e[1] + p[3] + sc_back(e[5] + p[6]))
        inv[at] = jnp.where(low > 0.0, 1.0 / total, 0.0)
        return 0

    lax.fori_loop(1, last, diag_step, 0)

    def sweep(field, first, end, put):
        def upward(c, at, v):
            high = field[c, at + 1]
            high_l = sl(high)
            high_s = sc(high)
            high_ls = sc(high_l)
            moved[c, 0], moved[c, 1], moved[c, 2] = high_l, high_s, high_ls
            return (
                coef[0, at] * (high - v),
                coef[3, at] * (high_l - v),
                coef[4, at] * (high_s - v),
                coef[6, at] * (high_ls - v),
            )

        for c in range(COMP):
            fluxes = upward(c, first - 1, field[c, first - 1])
            for k in range(4):
                carry[c, k] = fluxes[k]

        def step(at, _):
            low_n = n[at] * rim
            invd = inv[at]
            for c in range(COMP):
                v = field[c, at]
                f1 = coef[1, at] * (moved[c, 0] - v)
                f2 = coef[2, at] * (moved[c, 1] - v)
                f5 = coef[5, at] * (moved[c, 2] - v)
                f0, f3, f4, f6 = upward(c, at, v)
                inward = sc_back(f2 + carry[c, 2])
                inward = inward + sl_back(f1 + carry[c, 1] + sc_back(f5 + carry[c, 3]))
                inward = inward + carry[c, 0]
                total = ((f0 + f1) + (f2 + f3)) + ((f4 + f5) + f6)
                carry[c, 0], carry[c, 1], carry[c, 2], carry[c, 3] = f0, f3, f4, f6
                total = (total - inward) + (force[c, at] - low_n * v)
                put(c, at, v, total * invd)
            return 0

        lax.fori_loop(first, end, step, 0)

    def put1(c, at, v, change):
        u1[c, at] = v + OMEGA * change

    def put2(c, at, v, change):
        u2[c, at] = v + OMEGA * change

    def put3(c, at, v, change):
        u0[c, at] = change

    sweep(u0, 1, last, put1)
    sweep(u1, 2, last - 1, put2)
    smoothed[...] = u2[:, own, main]
    sweep(u2, 3, last - 2, put3)

    for c in range(COMP):
        for i in range(rows // 2):
            at = BELOW + 2 * i
            restr[c * (rows // 2) + i] = 0.25 * (u0[c, at] + u0[c, at + 2]) + 0.5 * u0[c, at + 1]
    parts = []
    for i in range(COMP * (rows // 2)):
        a = restr[i, pl.ds(0, cols // 2, stride=2)]
        b = restr[i, pl.ds(1, cols // 2, stride=2)]
        d = restr[i, pl.ds(2, cols // 2, stride=2)]
        parts.append(0.25 * (a + d) + 0.5 * b)
    source = lax.broadcasted_iota(jnp.int32, (lanes, lanes // 2), 0)
    target = 2 * lax.broadcasted_iota(jnp.int32, (lanes, lanes // 2), 1)
    gap = source - target
    h = jnp.where(gap == 1, 0.5, jnp.where((gap == 0) | (gap == 2), 0.25, 0.0))
    for c in range(COMP):
        block = jnp.concatenate(parts[c * (rows // 2) : (c + 1) * (rows // 2)], 0)
        out = jnp.dot(block, h, precision=lax.Precision.HIGHEST, preferred_element_type=jnp.float32)
        coarse[c] = out.reshape(rows // 2, cols // 2, lanes // 2)


def smooth(wts, u, rhs, visc, left, right, above, below, above_c, below_c):
    rows, cols, lanes = visc.shape
    deep, wide = rows + BELOW + ABOVE, cols + TILE
    f32 = jnp.float32
    vmem = pl.BlockSpec(memory_space=pltpu.VMEM)
    return pl.pallas_call(
        smooth_kernel,
        out_shape=[
            jax.ShapeDtypeStruct(u.shape, f32),
            jax.ShapeDtypeStruct((COMP, rows // 2, cols // 2, lanes // 2), f32),
        ],
        in_specs=[pl.BlockSpec(memory_space=pltpu.SMEM)] + [vmem] * 9,
        out_specs=[vmem] * 2,
        scratch_shapes=[
            pltpu.VMEM((COMP, deep, wide, lanes), f32),
            pltpu.VMEM((COMP, deep, wide, lanes), f32),
            pltpu.VMEM((COMP, deep, wide, lanes), f32),
            pltpu.VMEM((COMP, deep, wide, lanes), f32),
            pltpu.VMEM((deep, wide, lanes), f32),
            pltpu.VMEM((7, deep, wide, lanes), f32),
            pltpu.VMEM((deep, wide, lanes), f32),
            pltpu.VMEM((COMP, 4, wide, lanes), f32),
            pltpu.VMEM((COMP, 3, wide, lanes), f32),
            pltpu.VMEM((COMP * (rows // 2), wide, lanes), f32),
        ],
        compiler_params=pltpu.CompilerParams(vmem_limit_bytes=32 << 20),
        cost_estimate=pl.CostEstimate(flops=50_000_000, bytes_accessed=4 << 20, transcendentals=0),
        name="smooth",
    )(wts, u, rhs, visc, left, right, above, below, above_c, below_c)


def sent(value, axis, steps):
    count = lax.axis_size(axis)
    pairs = [(i, i + steps) for i in range(count) if 0 <= i + steps < count]
    return lax.ppermute(value, axis, pairs)


def per_device(solution, right_side, viscosity, stencil_weights):
    to_below, to_above, to_left, to_right = pack(solution, right_side, viscosity)
    above = sent(to_below, "shell", -1)
    below = sent(to_above, "shell", 1)
    right = sent(to_left, "lat", -1)
    left = sent(to_right, "lat", 1)
    to_below_c, to_above_c = corners(left, right)
    above_c = sent(to_below_c, "shell", -1)
    below_c = sent(to_above_c, "shell", 1)
    return smooth(
        stencil_weights, solution, right_side, viscosity, left, right, above, below, above_c, below_c
    )


def solution(mesh):
    in_specs = (
        P(None, "shell", "lat", None),
        P(None, "shell", "lat", None),
        P("shell", "lat", None),
        P(),
    )
    out_specs = (P(None, "shell", "lat", None), P(None, "shell", "lat", None))
    return jax.shard_map(
        per_device, mesh=mesh, in_specs=in_specs, out_specs=out_specs, check_vma=False
    )
```

```python
import jax
import jax.numpy as jnp
from jax import lax
from jax.experimental import pallas as pl
from jax.experimental.pallas import tpu as pltpu
from jax.sharding import PartitionSpec as P

OMEGA = 0.6
COMP = 3
BELOW = 3
ABOVE = 4
TILE = 8


def pack_kernel(u, rhs, visc, to_below, to_above, to_left, to_right, sems):
    rows, cols = visc.shape[0], visc.shape[1]
    copies = []

    def copy(src, dst):
        copies.append(pltpu.make_async_copy(src, dst, sems.at[len(copies)]))
        copies[-1].start()

    def rows_of(buffer, count, first_n, first_r, count_r):
        at = 0
        for c in range(COMP):
            copy(u.at[c, pl.ds(first_n, count)], buffer.at[pl.ds(at, count)])
            at += count
        copy(visc.at[pl.ds(first_n, count)], buffer.at[pl.ds(at, count)])
        at += count
        for c in range(COMP):
            copy(rhs.at[c, pl.ds(first_r, count_r)], buffer.at[pl.ds(at, count_r)])
            at += count_r

    rows_of(to_below, ABOVE, 0, 0, ABOVE - 1)
    rows_of(to_above, BELOW, rows - BELOW, rows - BELOW + 1, BELOW - 1)
    for buffer, first in ((to_left, 0), (to_right, cols - TILE)):
        copy(u.at[:, :, pl.ds(first, TILE)], buffer.at[pl.ds(0, COMP)])
        copy(rhs.at[:, :, pl.ds(first, TILE)], buffer.at[pl.ds(COMP, COMP)])
        copy(visc.at[:, pl.ds(first, TILE)], buffer.at[2 * COMP])
    for each in copies:
        each.wait()


def pack(u, rhs, visc):
    rows, cols, lanes = visc.shape
    f32 = jnp.float32
    shapes = (
        ((4 * ABOVE + 3 * (ABOVE - 1)), cols, lanes),
        ((4 * BELOW + 3 * (BELOW - 1)), cols, lanes),
        (2 * COMP + 1, rows, TILE, lanes),
        (2 * COMP + 1, rows, TILE, lanes),
    )
    return pl.pallas_call(
        pack_kernel,
        out_shape=[jax.ShapeDtypeStruct(s, f32) for s in shapes],
        in_specs=[pl.BlockSpec(memory_space=pltpu.HBM)] * 3,
        out_specs=[pl.BlockSpec(memory_space=pltpu.VMEM)] * 4,
        scratch_shapes=[pltpu.SemaphoreType.DMA((20,))],
        compiler_params=pltpu.CompilerParams(vmem_limit_bytes=8 << 20),
        cost_estimate=pl.CostEstimate(flops=0, bytes_accessed=4 << 20, transcendentals=0),
        name="pack",
    )(*(pltpu.with_memory_space_constraint(x, pltpu.HBM) for x in (u, rhs, visc)))


def corner_kernel(left, right, to_below, to_above):
    rows = left.shape[1]
    late = lax.broadcasted_iota(jnp.int32, left.shape[2:], 0) >= TILE - BELOW

    def rows_of(buffer, count, first_n, first_r, count_r):
        at = 0
        picks = [(c, first_n + i) for c in range(COMP) for i in range(count)]
        picks += [(2 * COMP, first_n + i) for i in range(count)]
        picks += [(COMP + c, first_r + i) for c in range(COMP) for i in range(count_r)]
        for field, row in picks:
            buffer[at] = jnp.where(late, left[field, row], right[field, row])
            at += 1

    rows_of(to_below, ABOVE, 0, 0, ABOVE - 1)
    rows_of(to_above, BELOW, rows - BELOW, rows - BELOW + 1, BELOW - 1)


def corners(left, right):
    lanes = left.shape[-1]
    shapes = (
        ((4 * ABOVE + 3 * (ABOVE - 1)), TILE, lanes),
        ((4 * BELOW + 3 * (BELOW - 1)), TILE, lanes),
    )
    return pl.pallas_call(
        corner_kernel,
        out_shape=[jax.ShapeDtypeStruct(s, jnp.float32) for s in shapes],
        in_specs=[pl.BlockSpec(memory_space=pltpu.VMEM)] * 2,
        out_specs=[pl.BlockSpec(memory_space=pltpu.VMEM)] * 2,
        compiler_params=pltpu.CompilerParams(vmem_limit_bytes=8 << 20),
        cost_estimate=pl.CostEstimate(flops=0, bytes_accessed=1 << 20, transcendentals=0),
        name="corners",
    )(left, right)


def smooth_kernel(
    wts, u, rhs, visc, left, right, above, below, above_c, below_c,
    smoothed, coarse,
    a, b, force, n, coef, inv, restr,
):
    rows, cols, lanes = visc.shape
    wide = cols + TILE
    tiles = wide // TILE
    late = lax.broadcasted_iota(jnp.int32, (TILE, lanes), 0) >= TILE - BELOW
    lane = lax.broadcasted_iota(jnp.int32, (TILE, lanes), 1)

    def part(ref, at, t, shift=0):
        return ref[(*at, pl.ds(TILE * (t + 1) + shift, TILE))]

    def put(ref, at, t, value):
        ref[(*at, pl.ds(TILE * (t + 1), TILE))] = value

    def put_round(ref, at, t, value):
        put(ref, at, t, value)
        if t == 0:
            put(ref, at, tiles, value)
        if t == tiles - 1:
            put(ref, at, -1, value)

    def ahead(x):
        return pltpu.roll(x, lanes - 1, 1)

    def behind(x):
        return pltpu.roll(x, 1, 1)

    def lay(ref, at, main, side):
        for t in range(tiles - 1):
            put_round(ref, at, t, main(t))
        put_round(ref, at, tiles - 1, side)

    def lay_force(c, at, main, side):
        for t in range(tiles - 1):
            force[c, at, pl.ds(TILE * t, TILE)] = main(t)
        force[c, at, pl.ds(cols, TILE)] = side

    def of(ref, *at):
        return lambda t: ref[(*at, pl.ds(TILE * t, TILE))]

    def own_step(r, _):
        at = r + BELOW
        for c in range(COMP):
            lay(a, (c, at), of(u, c, r), jnp.where(late, left[c, r], right[c, r]))
            lay_force(c, at, of(rhs, c, r), jnp.where(late, left[COMP + c, r], right[COMP + c, r]))
        lay(n, (at,), of(visc, r), jnp.where(late, left[2 * COMP, r], right[2 * COMP, r]))
        return 0

    def halo(main, side, first, count, first_r, count_r):
        def step(i, _):
            for c in range(COMP):
                lay(a, (c, first + i), of(main, c * count + i), side[c * count + i])
            lay(n, (first + i,), of(main, COMP * count + i), side[COMP * count + i])
            return 0

        def step_r(i, _):
            for c in range(COMP):
                j = (COMP + 1) * count + c * count_r + i
                lay_force(c, first_r + i, of(main, j), side[j])
            return 0

        lax.fori_loop(0, count, step, 0)
        lax.fori_loop(0, count_r, step_r, 0)

    lax.fori_loop(0, rows, own_step, 0)
    halo(above, above_c, BELOW + rows, ABOVE, BELOW + rows, ABOVE - 1)
    halo(below, below_c, 0, BELOW, 1, BELOW - 1)

    plain = ((1, 0, 0), (0, 1, 1), (1, 1, 3), (-1, 0, 0), (0, -1, 1), (-1, -1, 3))
    from_next = ((0, 0, 2), (1, 0, 4), (0, 1, 5), (1, 1, 6))
    from_prev = ((0, 0, 2), (-1, 0, 4), (0, -1, 5), (-1, -1, 6))
    groups = (plain, from_next, from_prev)

    half = [0.5 * wts[k] for k in range(7)]
    lost = half[2] + half[4] + half[5] + half[6]
    rim = jnp.where((lane == 0) | (lane == lanes - 1), lost, 0.0)
    weight = [[half[k] for _, _, k in plain]]
    weight += [[jnp.where(lane > 0, half[k], 0.0) for _, _, k in from_next]]
    weight += [[jnp.where(lane < lanes - 1, half[k], 0.0) for _, _, k in from_prev]]

    def total(terms):
        while len(terms) > 1:
            terms = [sum(terms[i : i + 2]) for i in range(0, len(terms), 2)]
        return terms[0]

    def coef_step(at, _):
        for t in range(tiles):
            here = part(n, (at,), t)
            sums, j = [], 0
            for group, own, ws in zip(groups, (here, behind(here), ahead(here)), weight):
                cs = []
                for (up, side, _), w in zip(group, ws):
                    cs.append(w * (own + part(n, (at + up,), t, side)))
                    coef[j, at, pl.ds(TILE * t, TILE)] = cs[-1]
                    j += 1
                sums.append(total(cs))
            diag = (sums[0] + rim * here) + (ahead(sums[1]) + behind(sums[2]))
            inv[at, pl.ds(TILE * t, TILE)] = jnp.where(here > 0.0, 1.0 / diag, 0.0)
        return 0

    last = BELOW + rows + ABOVE - 1
    lax.fori_loop(1, last, coef_step, 0, unroll=2)

    def sweep(field, first, end, store):
        def step(at, _):
            for t in range(tiles):
                here = pl.ds(TILE * t, TILE)
                cs = [coef[j, at, here] for j in range(14)]
                invd = inv[at, here]
                for c in range(COMP):
                    sums, j = [], 0
                    for group in groups:
                        terms = []
                        for up, side, _ in group:
                            terms.append(cs[j] * part(field, (c, at + up), t, side))
                            j += 1
                        sums.append(total(terms))
                    target = (sums[0] + force[c, at, here]) + (ahead(sums[1]) + behind(sums[2]))
                    store(c, at, t, part(field, (c, at), t), target * invd)
            return 0

        lax.fori_loop(first, end, step, 0, unroll=3)

    def store1(c, at, t, v, target):
        put_round(b, (c, at), t, (1.0 - OMEGA) * v + OMEGA * target)

    def store2(c, at, t, v, target):
        put_round(a, (c, at), t, (1.0 - OMEGA) * v + OMEGA * target)

    def store3(c, at, t, v, target):
        b[c, at, pl.ds(TILE * (t + 1), TILE)] = target - v

    sweep(a, 1, last, store1)
    sweep(b, 2, last - 1, store2)
    smoothed[...] = a[:, BELOW : BELOW + rows, TILE : TILE + cols]
    sweep(a, 3, last - 2, store3)

    for c in range(COMP):
        for i in range(rows // 2):
            at = BELOW + 2 * i
            restr[c * (rows // 2) + i] = 0.25 * (b[c, at, TILE:] + b[c, at + 2, TILE:]) + 0.5 * b[c, at + 1, TILE:]
    parts = []
    for i in range(COMP * (rows // 2)):
        p = restr[i, pl.ds(0, cols // 2, stride=2)]
        q = restr[i, pl.ds(1, cols // 2, stride=2)]
        d = restr[i, pl.ds(2, cols // 2, stride=2)]
        parts.append(0.25 * (p + d) + 0.5 * q)
    source = lax.broadcasted_iota(jnp.int32, (lanes, lanes // 2), 0)
    target = 2 * lax.broadcasted_iota(jnp.int32, (lanes, lanes // 2), 1)
    gap = source - target
    h = jnp.where(gap == 1, 0.5, jnp.where((gap == 0) | (gap == 2), 0.25, 0.0))
    for c in range(COMP):
        block = jnp.concatenate(parts[c * (rows // 2) : (c + 1) * (rows // 2)], 0)
        out = jnp.dot(block, h, precision=lax.Precision.HIGHEST, preferred_element_type=jnp.float32)
        coarse[c] = out.reshape(rows // 2, cols // 2, lanes // 2)


def smooth(wts, u, rhs, visc, left, right, above, below, above_c, below_c):
    rows, cols, lanes = visc.shape
    deep, wide = rows + BELOW + ABOVE, cols + TILE
    f32 = jnp.float32
    vmem = pl.BlockSpec(memory_space=pltpu.VMEM)
    padded = wide + 2 * TILE
    return pl.pallas_call(
        smooth_kernel,
        out_shape=[
            jax.ShapeDtypeStruct(u.shape, f32),
            jax.ShapeDtypeStruct((COMP, rows // 2, cols // 2, lanes // 2), f32),
        ],
        in_specs=[pl.BlockSpec(memory_space=pltpu.SMEM)] + [vmem] * 9,
        out_specs=[vmem] * 2,
        scratch_shapes=[pltpu.VMEM((COMP, deep, padded, lanes), f32)] * 2
        + [pltpu.VMEM((COMP, deep, wide, lanes), f32)]
        + [pltpu.VMEM((deep, padded, lanes), f32)]
        + [
            pltpu.VMEM((14, deep, wide, lanes), f32),
            pltpu.VMEM((deep, wide, lanes), f32),
            pltpu.VMEM((COMP * (rows // 2), wide + TILE, lanes), f32),
        ],
        compiler_params=pltpu.CompilerParams(vmem_limit_bytes=24 << 20),
        cost_estimate=pl.CostEstimate(flops=50_000_000, bytes_accessed=4 << 20, transcendentals=0),
        name="smooth",
    )(wts, u, rhs, visc, left, right, above, below, above_c, below_c)


def sent(value, axis, steps):
    count = lax.axis_size(axis)
    pairs = [(i, i + steps) for i in range(count) if 0 <= i + steps < count]
    return lax.ppermute(value, axis, pairs)


def per_device(solution, right_side, viscosity, stencil_weights):
    to_below, to_above, to_left, to_right = pack(solution, right_side, viscosity)
    above = sent(to_below, "shell", -1)
    right = sent(to_left, "lat", -1)
    left = sent(to_right, "lat", 1)
    below = sent(to_above, "shell", 1)
    to_below_c, to_above_c = corners(left, right)
    above_c = sent(to_below_c, "shell", -1)
    below_c = sent(to_above_c, "shell", 1)
    return smooth(
        stencil_weights, solution, right_side, viscosity, left, right, above, below, above_c, below_c
    )


def solution(mesh):
    in_specs = (
        P(None, "shell", "lat", None),
        P(None, "shell", "lat", None),
        P("shell", "lat", None),
        P(),
    )
    out_specs = (P(None, "shell", "lat", None), P(None, "shell", "lat", None))
    return jax.shard_map(
        per_device, mesh=mesh, in_specs=in_specs, out_specs=out_specs, check_vma=False
    )
```

```python
import jax
import jax.numpy as jnp
from jax import lax
from jax.experimental import pallas as pl
from jax.experimental.pallas import tpu as pltpu
from jax.sharding import PartitionSpec as P

OMEGA = 0.6
COMP = 3
BELOW = 3
ABOVE = 4
TILE = 8


def turned(x):
    return pltpu.roll(x, TILE // 2, 0)


def row_of(ref, field, pair, odd):
    return turned(ref[field, pair]) if odd else ref[field, pair]


def pack_kernel(u, rhs, visc, to_left, to_right, to_below, to_above, first_cols, last_cols, sems):
    rows, cols, lanes = visc.shape
    pairs = []
    for buffer, first in ((first_cols, 0), (last_cols, cols - TILE)):
        pairs.append((u.at[:, :, pl.ds(first, TILE)], buffer.at[pl.ds(0, COMP)]))
        pairs.append((rhs.at[:, :, pl.ds(first, TILE)], buffer.at[pl.ds(COMP, COMP)]))
        pairs.append((visc.at[:, pl.ds(first, TILE)], buffer.at[2 * COMP]))
    for buffer, count, first in ((to_below, ABOVE, 0), (to_above, BELOW, rows - BELOW)):
        short, first_r = count - 1, first if first == 0 else first + 1
        for c in range(COMP):
            pairs.append((u.at[c, pl.ds(first, count)], buffer.at[pl.ds(c * count, count)]))
        pairs.append((visc.at[pl.ds(first, count)], buffer.at[pl.ds(COMP * count, count)]))
        for c in range(COMP):
            at = (COMP + 1) * count + c * short
            pairs.append((rhs.at[c, pl.ds(first_r, short)], buffer.at[pl.ds(at, short)]))
    copies = [pltpu.make_async_copy(src, dst, sems.at[i]) for i, (src, dst) in enumerate(pairs)]
    for each in copies:
        each.start()
    for each in copies[:6]:
        each.wait()
    low = lax.broadcasted_iota(jnp.int32, (TILE, lanes), 0) < TILE // 2
    for field in range(2 * COMP + 1):
        for i in range(rows // 2):
            a, b = first_cols[field, 2 * i], first_cols[field, 2 * i + 1]
            to_left[field, i] = jnp.where(low, a, turned(b))
            a, b = last_cols[field, 2 * i], last_cols[field, 2 * i + 1]
            to_right[field, i] = jnp.where(low, turned(b), a)
    for each in copies[6:]:
        each.wait()


def shell_rows(count):
    return (COMP + 1) * count + COMP * (count - 1)


def pack(u, rhs, visc):
    rows, cols, lanes = visc.shape
    shapes = ((2 * COMP + 1, rows // 2, TILE, lanes),) * 2
    shapes += ((shell_rows(ABOVE), cols, lanes), (shell_rows(BELOW), cols, lanes))
    return pl.pallas_call(
        pack_kernel,
        out_shape=[jax.ShapeDtypeStruct(s, jnp.float32) for s in shapes],
        in_specs=[pl.BlockSpec(memory_space=pltpu.HBM)] * 3,
        out_specs=[pl.BlockSpec(memory_space=pltpu.VMEM)] * 4,
        scratch_shapes=[pltpu.VMEM((2 * COMP + 1, rows, TILE, lanes), jnp.float32)] * 2
        + [pltpu.SemaphoreType.DMA((20,))],
        compiler_params=pltpu.CompilerParams(vmem_limit_bytes=8 << 20),
        cost_estimate=pl.CostEstimate(flops=0, bytes_accessed=4 << 20, transcendentals=0),
        name="pack",
    )(*(pltpu.with_memory_space_constraint(x, pltpu.HBM) for x in (u, rhs, visc)))


def held(value, until):
    anywhere = pl.BlockSpec(memory_space=pl.ANY)
    return pl.pallas_call(
        lambda *_: None,
        out_shape=jax.ShapeDtypeStruct(value.shape, value.dtype),
        in_specs=[anywhere] * 2,
        out_specs=anywhere,
        input_output_aliases={0: 0},
        cost_estimate=pl.CostEstimate(flops=0, bytes_accessed=1024, transcendentals=0),
        name="held",
    )(value, until)


def corner_kernel(left, right, to_below, to_above):
    rows = 2 * left.shape[1]
    late = lax.broadcasted_iota(jnp.int32, left.shape[2:], 0) >= TILE - BELOW

    def rows_of(buffer, count, first_n, first_r, count_r):
        at = 0
        picks = [(c, first_n + i) for c in range(COMP) for i in range(count)]
        picks += [(2 * COMP, first_n + i) for i in range(count)]
        picks += [(COMP + c, first_r + i) for c in range(COMP) for i in range(count_r)]
        for field, row in picks:
            buffer[at] = jnp.where(
                late, row_of(left, field, row // 2, row % 2), row_of(right, field, row // 2, row % 2)
            )
            at += 1

    rows_of(to_below, ABOVE, 0, 0, ABOVE - 1)
    rows_of(to_above, BELOW, rows - BELOW, rows - BELOW + 1, BELOW - 1)


def corners(left, right):
    lanes = left.shape[-1]
    shapes = (
        ((4 * ABOVE + 3 * (ABOVE - 1)), TILE, lanes),
        ((4 * BELOW + 3 * (BELOW - 1)), TILE, lanes),
    )
    return pl.pallas_call(
        corner_kernel,
        out_shape=[jax.ShapeDtypeStruct(s, jnp.float32) for s in shapes],
        in_specs=[pl.BlockSpec(memory_space=pltpu.VMEM)] * 2,
        out_specs=[pl.BlockSpec(memory_space=pltpu.VMEM)] * 2,
        compiler_params=pltpu.CompilerParams(vmem_limit_bytes=8 << 20),
        cost_estimate=pl.CostEstimate(flops=0, bytes_accessed=1 << 20, transcendentals=0),
        name="corners",
    )(left, right)


def stencil_parts(wts, a, b, force, n, coef, inv):
    wide, lanes = coef.shape[-2:]
    tiles = wide // TILE
    lane = lax.broadcasted_iota(jnp.int32, (TILE, lanes), 1)

    def over(step, spans):
        for first, end in spans:
            unroll = 3 if (end - first) % 3 == 0 else 2 if (end - first) % 2 == 0 else end - first
            lax.fori_loop(first, end, step, 0, unroll=unroll)

    def part(ref, at, t, shift=0):
        return ref[(*at, pl.ds(TILE * (t + 1) + shift, TILE))]

    def put(ref, at, t, value):
        ref[(*at, pl.ds(TILE * (t + 1), TILE))] = value

    def put_round(ref, at, t, value):
        put(ref, at, t, value)
        if t == 0:
            put(ref, at, tiles, value)
        if t == tiles - 1:
            put(ref, at, -1, value)

    def ahead(x):
        return pltpu.roll(x, lanes - 1, 1)

    def behind(x):
        return pltpu.roll(x, 1, 1)

    def lay(ref, at, main, side):
        for t in range(tiles - 1):
            put_round(ref, at, t, main(t))
        put_round(ref, at, tiles - 1, side)

    def lay_force(c, at, main, side):
        for t in range(tiles - 1):
            force[c, at, pl.ds(TILE * t, TILE)] = main(t)
        force[c, at, pl.ds(TILE * (tiles - 1), TILE)] = side

    def of(ref, *at):
        return lambda t: ref[(*at, pl.ds(TILE * t, TILE))]

    plain = ((1, 0, 0), (0, 1, 1), (1, 1, 3), (-1, 0, 0), (0, -1, 1), (-1, -1, 3))
    from_next = ((0, 0, 2), (1, 0, 4), (0, 1, 5), (1, 1, 6))
    from_prev = ((0, 0, 2), (-1, 0, 4), (0, -1, 5), (-1, -1, 6))
    groups = (plain, from_next, from_prev)

    half = [0.5 * wts[k] for k in range(7)]
    lost = half[2] + half[4] + half[5] + half[6]
    rim = jnp.where((lane == 0) | (lane == lanes - 1), lost, 0.0)
    weight = [[half[k] for _, _, k in plain]]
    weight += [[jnp.where(lane > 0, half[k], 0.0) for _, _, k in from_next]]
    weight += [[jnp.where(lane < lanes - 1, half[k], 0.0) for _, _, k in from_prev]]

    def total(terms):
        while len(terms) > 1:
            terms = [sum(terms[i : i + 2]) for i in range(0, len(terms), 2)]
        return terms[0]

    def coef_step(at, _):
        for t in range(tiles):
            here = part(n, (at,), t)
            sums, j = [], 0
            for group, own, ws in zip(groups, (here, behind(here), ahead(here)), weight):
                cs = []
                for (up, side, _), w in zip(group, ws):
                    cs.append(w * (own + part(n, (at + up,), t, side)))
                    coef[j, at, pl.ds(TILE * t, TILE)] = cs[-1]
                    j += 1
                sums.append(total(cs))
            diag = (sums[0] + rim * here) + (ahead(sums[1]) + behind(sums[2]))
            inv[at, pl.ds(TILE * t, TILE)] = jnp.where(here > 0.0, 1.0 / diag, 0.0)
        return 0

    def coefs(*spans):
        over(coef_step, spans)

    def sweep(field, store, *spans):
        def step(at, _):
            for t in range(tiles):
                here = pl.ds(TILE * t, TILE)
                cs = [coef[j, at, here] for j in range(14)]
                invd = inv[at, here]
                for c in range(COMP):
                    sums, j = [], 0
                    for group in groups:
                        terms = []
                        for up, side, _ in group:
                            terms.append(cs[j] * part(field, (c, at + up), t, side))
                            j += 1
                        sums.append(total(terms))
                    target = (sums[0] + force[c, at, here]) + (ahead(sums[1]) + behind(sums[2]))
                    store(c, at, t, part(field, (c, at), t), target * invd)
            return 0

        over(step, spans)

    def store1(c, at, t, v, target):
        put_round(b, (c, at), t, (1.0 - OMEGA) * v + OMEGA * target)

    def store2(c, at, t, v, target):
        put_round(a, (c, at), t, (1.0 - OMEGA) * v + OMEGA * target)

    def store3(c, at, t, v, target):
        b[c, at, pl.ds(TILE * (t + 1), TILE)] = target - v

    return (
        lay,
        lay_force,
        of,
        coefs,
        lambda *spans: sweep(a, store1, *spans),
        lambda *spans: sweep(b, store2, *spans),
        lambda *spans: sweep(a, store3, *spans),
    )


def inner_kernel(wts, u, rhs, visc, left, right, _, a, b, force, n, coef, inv):
    rows, cols, lanes = visc.shape
    late = lax.broadcasted_iota(jnp.int32, (TILE, lanes), 0) >= TILE - BELOW
    lay, lay_force, of, coefs, sweep1, sweep2, residual = stencil_parts(wts, a, b, force, n, coef, inv)

    def own_step(i, _):
        for odd in range(2):
            r = 2 * i + odd
            at = r + BELOW

            def side(field):
                return jnp.where(late, row_of(left, field, i, odd), row_of(right, field, i, odd))

            for c in range(COMP):
                lay(a, (c, at), of(u, c, r), side(c))
                lay_force(c, at, of(rhs, c, r), side(COMP + c))
            lay(n, (at,), of(visc, r), side(2 * COMP))
        return 0

    first, end = BELOW, BELOW + rows
    lax.fori_loop(0, rows // 2, own_step, 0)
    coefs((first + 1, end - 1))
    sweep1((first + 1, end - 1))
    sweep2((first + 2, end - 2))
    residual((first + 3, end - 3))


def outer_kernel(
    wts, above, below, above_c, below_c, *refs
):
    a, b, force, n, coef, inv = refs[6:12]
    smoothed, coarse, restr, sems = refs[12:]
    rows, cols = smoothed.shape[1:3]
    lanes = smoothed.shape[3]
    lay, lay_force, of, coefs, sweep1, sweep2, residual = stencil_parts(wts, a, b, force, n, coef, inv)

    def halo(main, side, first, count, first_r, count_r):
        def step(i, _):
            for c in range(COMP):
                lay(a, (c, first + i), of(main, c * count + i), side[c * count + i])
            lay(n, (first + i,), of(main, COMP * count + i), side[COMP * count + i])
            return 0

        def step_r(i, _):
            for c in range(COMP):
                j = (COMP + 1) * count + c * count_r + i
                lay_force(c, first_r + i, of(main, j), side[j])
            return 0

        lax.fori_loop(0, count, step, 0)
        lax.fori_loop(0, count_r, step_r, 0)

    halo(above, above_c, BELOW + rows, ABOVE, BELOW + rows, ABOVE - 1)
    halo(below, below_c, 0, BELOW, 1, BELOW - 1)

    first, end = BELOW, BELOW + rows
    coefs((first - 2, first + 1), (end - 1, end + 3))
    sweep1((first - 2, first + 1), (end - 1, end + 3))
    sweep2((first - 1, first + 2), (end - 2, end + 2))
    copies = [
        pltpu.make_async_copy(a.at[c, pl.ds(first, rows), pl.ds(TILE, cols)], smoothed.at[c], sems.at[c])
        for c in range(COMP)
    ]
    for each in copies:
        each.start()
    residual((first, first + 3), (end - 3, end + 1))

    for c in range(COMP):
        for i in range(rows // 2):
            at = BELOW + 2 * i
            restr[c * (rows // 2) + i] = 0.25 * (b[c, at, TILE:] + b[c, at + 2, TILE:]) + 0.5 * b[c, at + 1, TILE:]
    parts = []
    for i in range(COMP * (rows // 2)):
        p = restr[i, pl.ds(0, cols // 2, stride=2)]
        q = restr[i, pl.ds(1, cols // 2, stride=2)]
        d = restr[i, pl.ds(2, cols // 2, stride=2)]
        parts.append(0.25 * (p + d) + 0.5 * q)
    source = lax.broadcasted_iota(jnp.int32, (lanes, lanes // 2), 0)
    target = 2 * lax.broadcasted_iota(jnp.int32, (lanes, lanes // 2), 1)
    gap = source - target
    h = jnp.where(gap == 1, 0.5, jnp.where((gap == 0) | (gap == 2), 0.25, 0.0))
    for c in range(COMP):
        block = jnp.concatenate(parts[c * (rows // 2) : (c + 1) * (rows // 2)], 0)
        out = jnp.dot(block, h, precision=lax.Precision.HIGHEST, preferred_element_type=jnp.float32)
        coarse[c] = out.reshape(rows // 2, cols // 2, lanes // 2)
    for each in copies:
        each.wait()


def state_shapes(rows, cols, lanes):
    deep, wide = rows + BELOW + ABOVE, cols + TILE
    padded = wide + 2 * TILE
    shapes = (
        (COMP, deep, padded, lanes),
        (COMP, deep, padded, lanes),
        (COMP, deep, wide, lanes),
        (deep, padded, lanes),
        (14, deep, wide, lanes),
        (deep, wide, lanes),
    )
    return [jax.ShapeDtypeStruct(s, jnp.float32) for s in shapes]


def inner(wts, u, rhs, visc, left, right, after):
    vmem = pl.BlockSpec(memory_space=pltpu.VMEM)
    return pl.pallas_call(
        inner_kernel,
        out_shape=state_shapes(*visc.shape),
        in_specs=[pl.BlockSpec(memory_space=pltpu.SMEM)] + [vmem] * 5 + [pl.BlockSpec(memory_space=pl.ANY)],
        out_specs=[vmem] * 6,
        compiler_params=pltpu.CompilerParams(vmem_limit_bytes=16 << 20),
        cost_estimate=pl.CostEstimate(flops=20_000_000, bytes_accessed=16 << 20, transcendentals=0),
        name="inner",
    )(wts, u, rhs, visc, left, right, after)


def outer(wts, above, below, above_c, below_c, state, rows, cols, lanes):
    vmem = pl.BlockSpec(memory_space=pltpu.VMEM)
    f32 = jnp.float32
    shapes = state_shapes(rows, cols, lanes)
    out = pl.pallas_call(
        outer_kernel,
        out_shape=shapes
        + [
            jax.ShapeDtypeStruct((COMP, rows, cols, lanes), f32),
            jax.ShapeDtypeStruct((COMP, rows // 2, cols // 2, lanes // 2), f32),
        ],
        in_specs=[pl.BlockSpec(memory_space=pltpu.SMEM)] + [vmem] * 10,
        out_specs=[vmem] * 6 + [pl.BlockSpec(memory_space=pltpu.HBM), vmem],
        input_output_aliases={5 + i: i for i in range(6)},
        scratch_shapes=[
            pltpu.VMEM((COMP * (rows // 2), cols + 2 * TILE, lanes), f32),
            pltpu.SemaphoreType.DMA((COMP,)),
        ],
        compiler_params=pltpu.CompilerParams(vmem_limit_bytes=16 << 20),
        cost_estimate=pl.CostEstimate(flops=40_000_000, bytes_accessed=16 << 20, transcendentals=0),
        name="outer",
    )(wts, above, below, above_c, below_c, *state)
    return out[6], out[7]


def sent(value, axis, steps):
    count = lax.axis_size(axis)
    pairs = [(i, i + steps) for i in range(count) if 0 <= i + steps < count]
    return lax.ppermute(value, axis, pairs)


def per_device(solution, right_side, viscosity, stencil_weights):
    to_left, to_right, to_below, to_above = pack(solution, right_side, viscosity)
    above = sent(to_below, "shell", -1)
    below = sent(to_above, "shell", 1)
    left = sent(to_right, "lat", 1)
    right = sent(to_left, "lat", -1)
    to_below_c, to_above_c = corners(left, right)
    above_c = sent(to_below_c, "shell", -1)
    below_c = sent(to_above_c, "shell", 1)
    state = inner(stencil_weights, solution, right_side, viscosity, left, right, to_below_c)
    return outer(stencil_weights, above, below, above_c, below_c, state, *viscosity.shape)


def solution(mesh):
    in_specs = (
        P(None, "shell", "lat", None),
        P(None, "shell", "lat", None),
        P("shell", "lat", None),
        P(),
    )
    out_specs = (P(None, "shell", "lat", None), P(None, "shell", "lat", None))
    return jax.shard_map(
        per_device, mesh=mesh, in_specs=in_specs, out_specs=out_specs, check_vma=False
    )
```

```python
import functools

import jax
import jax.numpy as jnp
from jax import lax
from jax.experimental import pallas as pl
from jax.experimental.pallas import tpu as pltpu
from jax.sharding import PartitionSpec as P

OMEGA = 0.6
COMP = 3
BELOW = 3
ABOVE = 4
TILE = 8


GROUPS = (
    ((1, 0, 0), (0, 1, 1), (1, 1, 3), (-1, 0, 0), (0, -1, 1), (-1, -1, 3)),
    ((0, 0, 2), (1, 0, 4), (0, 1, 5), (1, 1, 6)),
    ((0, 0, 2), (-1, 0, 4), (0, -1, 5), (-1, -1, 6)),
)


def turned(x):
    return pltpu.roll(x, TILE // 2, 0)


def row_of(ref, field, pair, odd):
    return turned(ref[field, pair]) if odd else ref[field, pair]


NEAR = 14


def pack_kernel(
    wts, u, rhs, visc, to_left, to_right, to_below, to_above, own_visc, weight, first_cols, last_cols, held, sems
):
    rows, cols, lanes = visc.shape
    pairs = []
    for buffer, first in ((first_cols, 0), (last_cols, cols - TILE)):
        pairs.append((u.at[:, :, pl.ds(first, TILE)], buffer.at[pl.ds(0, COMP)]))
        pairs.append((rhs.at[:, :, pl.ds(first, TILE)], buffer.at[pl.ds(COMP, COMP)]))
        pairs.append((visc.at[:, pl.ds(first, TILE)], buffer.at[2 * COMP]))
    for buffer, count, first in ((to_below, ABOVE, 0), (to_above, BELOW, rows - BELOW)):
        short, first_r = count - 1, first if first == 0 else first + 1
        for c in range(COMP):
            pairs.append((u.at[c, pl.ds(first, count)], buffer.at[pl.ds(c * count, count)]))
        pairs.append((visc.at[pl.ds(first, count)], buffer.at[pl.ds(COMP * count, count)]))
        for c in range(COMP):
            at = (COMP + 1) * count + c * short
            pairs.append((rhs.at[c, pl.ds(first_r, short)], buffer.at[pl.ds(at, short)]))
    pairs.append((wts, held))
    pairs.append((visc, own_visc))
    copies = [pltpu.make_async_copy(src, dst, sems.at[i]) for i, (src, dst) in enumerate(pairs)]
    for each in copies:
        each.start()
    for each in copies[:6]:
        each.wait()
    low = lax.broadcasted_iota(jnp.int32, (TILE, lanes), 0) < TILE // 2
    for field in range(2 * COMP + 1):
        for i in range(rows // 2):
            a, b = first_cols[field, 2 * i], first_cols[field, 2 * i + 1]
            to_left[field, i] = jnp.where(low, a, turned(b))
            a, b = last_cols[field, 2 * i], last_cols[field, 2 * i + 1]
            to_right[field, i] = jnp.where(low, turned(b), a)
    for each in copies[6:]:
        each.wait()
    lane = lax.broadcasted_iota(jnp.int32, (TILE, lanes), 1)
    half = [0.5 * held[k] for k in range(7)]
    j = 0
    for group, inside in zip(GROUPS, (lane >= 0, lane > 0, lane < lanes - 1)):
        for _, _, k in group:
            weight[j] = jnp.where(inside, half[k], 0.0)
            j += 1
    lost = half[2] + half[4] + half[5] + half[6]
    weight[j] = jnp.where((lane == 0) | (lane == lanes - 1), lost, 0.0)


def shell_rows(count):
    return (COMP + 1) * count + COMP * (count - 1)


def pack(wts, u, rhs, visc):
    rows, cols, lanes = visc.shape
    shapes = ((2 * COMP + 1, rows // 2, TILE, lanes),) * 2
    shapes += ((shell_rows(ABOVE), cols, lanes), (shell_rows(BELOW), cols, lanes))
    shapes += (visc.shape, (NEAR + 1, TILE, lanes))
    return pl.pallas_call(
        pack_kernel,
        out_shape=[jax.ShapeDtypeStruct(s, jnp.float32) for s in shapes],
        in_specs=[pl.BlockSpec(memory_space=pltpu.HBM)] * 4,
        out_specs=[pl.BlockSpec(memory_space=pltpu.VMEM)] * 6,
        scratch_shapes=[pltpu.VMEM((2 * COMP + 1, rows, TILE, lanes), jnp.float32)] * 2
        + [pltpu.SMEM((7,), jnp.float32), pltpu.SemaphoreType.DMA((22,))],
        compiler_params=pltpu.CompilerParams(vmem_limit_bytes=8 << 20),
        cost_estimate=pl.CostEstimate(flops=0, bytes_accessed=4 << 20, transcendentals=0),
        name="pack",
    )(*(pltpu.with_memory_space_constraint(x, pltpu.HBM) for x in (wts, u, rhs, visc)))


def corner_kernel(left, right, _, to_below, to_above):
    rows = 2 * left.shape[1]
    late = lax.broadcasted_iota(jnp.int32, left.shape[2:], 0) >= TILE - BELOW

    def rows_of(buffer, count, first_n, first_r, count_r):
        at = 0
        picks = [(c, first_n + i) for c in range(COMP) for i in range(count)]
        picks += [(2 * COMP, first_n + i) for i in range(count)]
        picks += [(COMP + c, first_r + i) for c in range(COMP) for i in range(count_r)]
        for field, row in picks:
            buffer[at] = jnp.where(
                late, row_of(left, field, row // 2, row % 2), row_of(right, field, row // 2, row % 2)
            )
            at += 1

    rows_of(to_below, ABOVE, 0, 0, ABOVE - 1)
    rows_of(to_above, BELOW, rows - BELOW, rows - BELOW + 1, BELOW - 1)


def corners(left, right, after):
    lanes = left.shape[-1]
    shapes = (
        ((4 * ABOVE + 3 * (ABOVE - 1)), TILE, lanes),
        ((4 * BELOW + 3 * (BELOW - 1)), TILE, lanes),
    )
    return pl.pallas_call(
        corner_kernel,
        out_shape=[jax.ShapeDtypeStruct(s, jnp.float32) for s in shapes],
        in_specs=[pl.BlockSpec(memory_space=pltpu.VMEM)] * 2 + [pl.BlockSpec(memory_space=pl.ANY)],
        out_specs=[pl.BlockSpec(memory_space=pltpu.VMEM)] * 2,
        compiler_params=pltpu.CompilerParams(vmem_limit_bytes=8 << 20),
        cost_estimate=pl.CostEstimate(flops=0, bytes_accessed=1 << 20, transcendentals=0),
        name="corners",
    )(left, right, after)


def stencil_parts(weight, a, b, force, n, coef, inv):
    wide, lanes = coef.shape[-2:]
    tiles = wide // TILE

    def over(step, spans):
        for first, end in spans:
            unroll = 3 if (end - first) % 3 == 0 else 2 if (end - first) % 2 == 0 else end - first

            def body(at, _):
                step(at)
                return 0

            lax.fori_loop(first, end, body, 0, unroll=unroll)

    def part(ref, at, t, shift=0):
        return ref[(*at, pl.ds(TILE * (t + 1) + shift, TILE))]

    def put(ref, at, t, value):
        ref[(*at, pl.ds(TILE * (t + 1), TILE))] = value

    def put_round(ref, at, t, value):
        put(ref, at, t, value)
        if t == 0:
            put(ref, at, tiles, value)
        if t == tiles - 1:
            put(ref, at, -1, value)

    def ahead(x):
        return pltpu.roll(x, lanes - 1, 1)

    def behind(x):
        return pltpu.roll(x, 1, 1)

    def lay(ref, at, main):
        for t in range(tiles - 1):
            put_round(ref, at, t, main(t))

    def lay_side(ref, at, side):
        put_round(ref, at, tiles - 1, side)

    def lay_force(c, at, main):
        for t in range(tiles - 1):
            force[c, at, pl.ds(TILE * t, TILE)] = main(t)

    def lay_force_side(c, at, side):
        force[c, at, pl.ds(TILE * (tiles - 1), TILE)] = side

    def of(ref, *at):
        return lambda t: ref[(*at, pl.ds(TILE * t, TILE))]

    def total(terms):
        while len(terms) > 1:
            terms = [sum(terms[i : i + 2]) for i in range(0, len(terms), 2)]
        return terms[0]

    def coef_row(at, chosen):
        for t in chosen:
            here = part(n, (at,), t)
            sums, j = [], 0
            for group, own in zip(GROUPS, (here, behind(here), ahead(here))):
                cs = []
                for up, side, _ in group:
                    cs.append(weight[j] * (own + part(n, (at + up,), t, side)))
                    coef[j, at, pl.ds(TILE * t, TILE)] = cs[-1]
                    j += 1
                sums.append(total(cs))
            diag = (sums[0] + weight[NEAR] * here) + (ahead(sums[1]) + behind(sums[2]))
            inv[at, pl.ds(TILE * t, TILE)] = jnp.where(here > 0.0, 1.0 / diag, 0.0)

    def coefs(spans, chosen=range(tiles)):
        over(lambda at: coef_row(at, chosen), spans)

    def sweep(field, store, spans, chosen=range(tiles)):
        def step(at):
            for t in chosen:
                here = pl.ds(TILE * t, TILE)
                cs = [coef[j, at, here] for j in range(NEAR)]
                invd = inv[at, here]
                for c in range(COMP):
                    sums, j = [], 0
                    for group in GROUPS:
                        terms = []
                        for up, side, _ in group:
                            terms.append(cs[j] * part(field, (c, at + up), t, side))
                            j += 1
                        sums.append(total(terms))
                    target = (sums[0] + force[c, at, here]) + (ahead(sums[1]) + behind(sums[2]))
                    store(c, at, t, part(field, (c, at), t), target * invd)

        over(step, spans)

    def store1(c, at, t, v, target):
        put_round(b, (c, at), t, (1.0 - OMEGA) * v + OMEGA * target)

    def store2(c, at, t, v, target):
        put_round(a, (c, at), t, (1.0 - OMEGA) * v + OMEGA * target)

    def store3(c, at, t, v, target):
        b[c, at, pl.ds(TILE * (t + 1), TILE)] = target - v

    return (
        (lay, lay_side, lay_force, lay_force_side, of),
        coefs,
        functools.partial(sweep, a, store1),
        functools.partial(sweep, b, store2),
        functools.partial(sweep, a, store3),
    )


def middle_kernel(weight, u, rhs, visc, a, b, force, n, coef, inv):
    rows, cols, _ = visc.shape
    laying, coefs, sweep1, sweep2, residual = stencil_parts(weight, a, b, force, n, coef, inv)
    lay, _, lay_force, _, of = laying

    def own_step(r, _):
        at = r + BELOW
        for c in range(COMP):
            lay(a, (c, at), of(u, c, r))
            lay_force(c, at, of(rhs, c, r))
        lay(n, (at,), of(visc, r))
        return 0

    first, end, last = BELOW, BELOW + rows, cols // TILE
    lax.fori_loop(0, rows, own_step, 0)
    coefs([(first + 1, end - 1)], range(1, last - 1))
    sweep1([(first + 1, end - 1)], range(1, last - 1))
    sweep2([(first + 2, end - 2)], range(2, last - 2))
    residual([(first + 3, end - 3)], range(3, last - 3))


def inner_kernel(weight, left, right, _, *refs):
    a, b, force, n, coef, inv = refs[6:]
    rows, lanes = 2 * left.shape[1], left.shape[3]
    late = lax.broadcasted_iota(jnp.int32, (TILE, lanes), 0) >= TILE - BELOW
    laying, coefs, sweep1, sweep2, residual = stencil_parts(weight, a, b, force, n, coef, inv)
    _, lay_side, _, lay_force_side, _ = laying

    def own_step(i, _):
        for odd in range(2):
            at = 2 * i + odd + BELOW

            def side(field):
                return jnp.where(late, row_of(left, field, i, odd), row_of(right, field, i, odd))

            for c in range(COMP):
                lay_side(a, (c, at), side(c))
                lay_force_side(c, at, side(COMP + c))
            lay_side(n, (at,), side(2 * COMP))
        return 0

    first, end, last = BELOW, BELOW + rows, inv.shape[1] // TILE - 1

    def rest(edge):
        return [t for t in range(last + 1) if not edge <= t < last - edge]

    lax.fori_loop(0, rows // 2, own_step, 0)
    coefs([(first + 1, end - 1)], rest(1))
    sweep1([(first + 1, end - 1)], rest(1))
    sweep2([(first + 2, end - 2)], rest(2))
    residual([(first + 3, end - 3)], rest(3))


def outer_kernel(
    weight, above, below, above_c, below_c, *refs
):
    a, b, force, n, coef, inv = refs[6:12]
    smoothed, coarse, restr, sems = refs[12:]
    rows, cols = smoothed.shape[1:3]
    lanes = smoothed.shape[3]
    laying, coefs, sweep1, sweep2, residual = stencil_parts(weight, a, b, force, n, coef, inv)
    lay, lay_side, lay_force, lay_force_side, of = laying

    def halo(main, side, first, count, first_r, count_r):
        def step(i, _):
            for c in range(COMP):
                lay(a, (c, first + i), of(main, c * count + i))
                lay_side(a, (c, first + i), side[c * count + i])
            lay(n, (first + i,), of(main, COMP * count + i))
            lay_side(n, (first + i,), side[COMP * count + i])
            return 0

        def step_r(i, _):
            for c in range(COMP):
                j = (COMP + 1) * count + c * count_r + i
                lay_force(c, first_r + i, of(main, j))
                lay_force_side(c, first_r + i, side[j])
            return 0

        lax.fori_loop(0, count, step, 0)
        lax.fori_loop(0, count_r, step_r, 0)

    halo(above, above_c, BELOW + rows, ABOVE, BELOW + rows, ABOVE - 1)
    halo(below, below_c, 0, BELOW, 1, BELOW - 1)

    first, end = BELOW, BELOW + rows
    coefs(((first - 2, first + 1), (end - 1, end + 3)))
    sweep1(((first - 2, first + 1), (end - 1, end + 3)))
    sweep2(((first - 1, first + 2), (end - 2, end + 2)))
    copies = [
        pltpu.make_async_copy(a.at[c, pl.ds(first, rows), pl.ds(TILE, cols)], smoothed.at[c], sems.at[c])
        for c in range(COMP)
    ]
    for each in copies:
        each.start()
    residual(((first, first + 3), (end - 3, end + 1)))

    for c in range(COMP):
        for i in range(rows // 2):
            at = BELOW + 2 * i
            restr[c * (rows // 2) + i] = 0.25 * (b[c, at, TILE:] + b[c, at + 2, TILE:]) + 0.5 * b[c, at + 1, TILE:]
    parts = []
    for i in range(COMP * (rows // 2)):
        p = restr[i, pl.ds(0, cols // 2, stride=2)]
        q = restr[i, pl.ds(1, cols // 2, stride=2)]
        d = restr[i, pl.ds(2, cols // 2, stride=2)]
        parts.append(0.25 * (p + d) + 0.5 * q)
    source = lax.broadcasted_iota(jnp.int32, (lanes, lanes // 2), 0)
    target = 2 * lax.broadcasted_iota(jnp.int32, (lanes, lanes // 2), 1)
    gap = source - target
    h = jnp.where(gap == 1, 0.5, jnp.where((gap == 0) | (gap == 2), 0.25, 0.0))
    for c in range(COMP):
        block = jnp.concatenate(parts[c * (rows // 2) : (c + 1) * (rows // 2)], 0)
        out = jnp.dot(block, h, precision=lax.Precision.HIGHEST, preferred_element_type=jnp.float32)
        coarse[c] = out.reshape(rows // 2, cols // 2, lanes // 2)
    for each in copies:
        each.wait()


def state_shapes(rows, cols, lanes):
    deep, wide = rows + BELOW + ABOVE, cols + TILE
    padded = wide + 2 * TILE
    shapes = (
        (COMP, deep, padded, lanes),
        (COMP, deep, padded, lanes),
        (COMP, deep, wide, lanes),
        (deep, padded, lanes),
        (14, deep, wide, lanes),
        (deep, wide, lanes),
    )
    return [jax.ShapeDtypeStruct(s, jnp.float32) for s in shapes]


def middle(weight, u, rhs, visc):
    vmem = pl.BlockSpec(memory_space=pltpu.VMEM)
    return pl.pallas_call(
        middle_kernel,
        out_shape=state_shapes(*visc.shape),
        in_specs=[vmem] * 4,
        out_specs=[vmem] * 6,
        compiler_params=pltpu.CompilerParams(vmem_limit_bytes=16 << 20),
        cost_estimate=pl.CostEstimate(flops=10_000_000, bytes_accessed=8 << 20, transcendentals=0),
        name="middle",
    )(weight, u, rhs, visc)


def inner(weight, left, right, after, state):
    vmem = pl.BlockSpec(memory_space=pltpu.VMEM)
    return pl.pallas_call(
        inner_kernel,
        out_shape=[jax.ShapeDtypeStruct(x.shape, x.dtype) for x in state],
        in_specs=[vmem] * 3 + [pl.BlockSpec(memory_space=pl.ANY)] + [vmem] * 6,
        out_specs=[vmem] * 6,
        input_output_aliases={4 + i: i for i in range(6)},
        compiler_params=pltpu.CompilerParams(vmem_limit_bytes=16 << 20),
        cost_estimate=pl.CostEstimate(flops=10_000_000, bytes_accessed=8 << 20, transcendentals=0),
        name="inner",
    )(weight, left, right, after, *state)


def outer(weight, above, below, above_c, below_c, state, rows, cols, lanes):
    vmem = pl.BlockSpec(memory_space=pltpu.VMEM)
    f32 = jnp.float32
    shapes = state_shapes(rows, cols, lanes)
    out = pl.pallas_call(
        outer_kernel,
        out_shape=shapes
        + [
            jax.ShapeDtypeStruct((COMP, rows, cols, lanes), f32),
            jax.ShapeDtypeStruct((COMP, rows // 2, cols // 2, lanes // 2), f32),
        ],
        in_specs=[vmem] * 11,
        out_specs=[vmem] * 6 + [pl.BlockSpec(memory_space=pltpu.HBM), vmem],
        input_output_aliases={5 + i: i for i in range(6)},
        scratch_shapes=[
            pltpu.VMEM((COMP * (rows // 2), cols + 2 * TILE, lanes), f32),
            pltpu.SemaphoreType.DMA((COMP,)),
        ],
        compiler_params=pltpu.CompilerParams(vmem_limit_bytes=16 << 20),
        cost_estimate=pl.CostEstimate(flops=40_000_000, bytes_accessed=16 << 20, transcendentals=0),
        name="outer",
    )(weight, above, below, above_c, below_c, *state)
    return out[6], out[7]


def sent(value, axis, steps):
    count = lax.axis_size(axis)
    pairs = [(i, i + steps) for i in range(count) if 0 <= i + steps < count]
    return lax.ppermute(value, axis, pairs)


def per_device(solution, right_side, viscosity, stencil_weights):
    to_left, to_right, to_below, to_above, own_visc, weight = pack(stencil_weights, solution, right_side, viscosity)
    above = sent(to_below, "shell", -1)
    below = sent(to_above, "shell", 1)
    left = sent(to_right, "lat", 1)
    right = sent(to_left, "lat", -1)
    state = middle(weight, solution, right_side, own_visc)
    to_below_c, to_above_c = corners(left, right, state[-1])
    above_c = sent(to_below_c, "shell", -1)
    below_c = sent(to_above_c, "shell", 1)
    state = inner(weight, left, right, to_below_c, state)
    return outer(weight, above, below, above_c, below_c, state, *viscosity.shape)


def solution(mesh):
    in_specs = (
        P(None, "shell", "lat", None),
        P(None, "shell", "lat", None),
        P("shell", "lat", None),
        P(),
    )
    out_specs = (P(None, "shell", "lat", None), P(None, "shell", "lat", None))
    return jax.shard_map(
        per_device, mesh=mesh, in_specs=in_specs, out_specs=out_specs, check_vma=False
    )
```

```python
import functools

import jax
import jax.numpy as jnp
from jax import lax
from jax.experimental import pallas as pl
from jax.experimental.pallas import tpu as pltpu
from jax.sharding import PartitionSpec as P

OMEGA = 0.6
COMP = 3
BELOW = 3
ABOVE = 4
TILE = 8


GROUPS = (
    ((1, 0, 0), (0, 1, 1), (1, 1, 3), (-1, 0, 0), (0, -1, 1), (-1, -1, 3)),
    ((0, 0, 2), (1, 0, 4), (0, 1, 5), (1, 1, 6)),
    ((0, 0, 2), (-1, 0, 4), (0, -1, 5), (-1, -1, 6)),
)


def turned(x):
    return pltpu.roll(x, TILE // 2, 0)


def row_of(ref, field, pair, odd):
    return turned(ref[field, pair]) if odd else ref[field, pair]


NEAR = 14


def pack_kernel(
    wts, u, rhs, visc, to_left, to_right, to_below, to_above, own_visc, weight, first_cols, last_cols, held, sems
):
    rows, cols, lanes = visc.shape
    pairs = []
    for buffer, first in ((first_cols, 0), (last_cols, cols - TILE)):
        pairs.append((u.at[:, :, pl.ds(first, TILE)], buffer.at[pl.ds(0, COMP)]))
        pairs.append((rhs.at[:, :, pl.ds(first, TILE)], buffer.at[pl.ds(COMP, COMP)]))
        pairs.append((visc.at[:, pl.ds(first, TILE)], buffer.at[2 * COMP]))
    for buffer, count, first in ((to_below, ABOVE, 0), (to_above, BELOW, rows - BELOW)):
        short, first_r = count - 1, first if first == 0 else first + 1
        for c in range(COMP):
            pairs.append((u.at[c, pl.ds(first, count)], buffer.at[pl.ds(c * count, count)]))
        pairs.append((visc.at[pl.ds(first, count)], buffer.at[pl.ds(COMP * count, count)]))
        for c in range(COMP):
            at = (COMP + 1) * count + c * short
            pairs.append((rhs.at[c, pl.ds(first_r, short)], buffer.at[pl.ds(at, short)]))
    pairs.append((wts, held))
    pairs.append((visc, own_visc))
    copies = [pltpu.make_async_copy(src, dst, sems.at[i]) for i, (src, dst) in enumerate(pairs)]
    for each in copies:
        each.start()
    for each in copies[:6]:
        each.wait()
    low = lax.broadcasted_iota(jnp.int32, (TILE, lanes), 0) < TILE // 2
    for field in range(2 * COMP + 1):
        for i in range(rows // 2):
            a, b = first_cols[field, 2 * i], first_cols[field, 2 * i + 1]
            to_left[field, i] = jnp.where(low, a, turned(b))
            a, b = last_cols[field, 2 * i], last_cols[field, 2 * i + 1]
            to_right[field, i] = jnp.where(low, turned(b), a)
    for each in copies[6:]:
        each.wait()
    lane = lax.broadcasted_iota(jnp.int32, (TILE, lanes), 1)
    half = [0.5 * held[k] for k in range(7)]
    j = 0
    for group, inside in zip(GROUPS, (lane >= 0, lane > 0, lane < lanes - 1)):
        for _, _, k in group:
            weight[j] = jnp.where(inside, half[k], 0.0)
            j += 1
    lost = half[2] + half[4] + half[5] + half[6]
    weight[j] = jnp.where((lane == 0) | (lane == lanes - 1), lost, 0.0)


def shell_rows(count):
    return (COMP + 1) * count + COMP * (count - 1)


def pack(wts, u, rhs, visc):
    rows, cols, lanes = visc.shape
    shapes = ((2 * COMP + 1, rows // 2, TILE, lanes),) * 2
    shapes += ((shell_rows(ABOVE), cols, lanes), (shell_rows(BELOW), cols, lanes))
    shapes += (visc.shape, (NEAR + 1, TILE, lanes))
    return pl.pallas_call(
        pack_kernel,
        out_shape=[jax.ShapeDtypeStruct(s, jnp.float32) for s in shapes],
        in_specs=[pl.BlockSpec(memory_space=pltpu.HBM)] * 4,
        out_specs=[pl.BlockSpec(memory_space=pltpu.VMEM)] * 6,
        scratch_shapes=[pltpu.VMEM((2 * COMP + 1, rows, TILE, lanes), jnp.float32)] * 2
        + [pltpu.SMEM((7,), jnp.float32), pltpu.SemaphoreType.DMA((22,))],
        compiler_params=pltpu.CompilerParams(vmem_limit_bytes=8 << 20),
        cost_estimate=pl.CostEstimate(flops=0, bytes_accessed=4 << 20, transcendentals=0),
        name="pack",
    )(*(pltpu.with_memory_space_constraint(x, pltpu.HBM) for x in (wts, u, rhs, visc)))


def corner_kernel(left, right, _, to_below, to_above):
    rows = 2 * left.shape[1]
    late = lax.broadcasted_iota(jnp.int32, left.shape[2:], 0) >= TILE - BELOW

    def rows_of(buffer, count, first_n, first_r, count_r):
        at = 0
        picks = [(c, first_n + i) for c in range(COMP) for i in range(count)]
        picks += [(2 * COMP, first_n + i) for i in range(count)]
        picks += [(COMP + c, first_r + i) for c in range(COMP) for i in range(count_r)]
        for field, row in picks:
            buffer[at] = jnp.where(
                late, row_of(left, field, row // 2, row % 2), row_of(right, field, row // 2, row % 2)
            )
            at += 1

    rows_of(to_below, ABOVE, 0, 0, ABOVE - 1)
    rows_of(to_above, BELOW, rows - BELOW, rows - BELOW + 1, BELOW - 1)


def corners(left, right, after):
    lanes = left.shape[-1]
    shapes = (
        ((4 * ABOVE + 3 * (ABOVE - 1)), TILE, lanes),
        ((4 * BELOW + 3 * (BELOW - 1)), TILE, lanes),
    )
    return pl.pallas_call(
        corner_kernel,
        out_shape=[jax.ShapeDtypeStruct(s, jnp.float32) for s in shapes],
        in_specs=[pl.BlockSpec(memory_space=pltpu.VMEM)] * 2 + [pl.BlockSpec(memory_space=pl.ANY)],
        out_specs=[pl.BlockSpec(memory_space=pltpu.VMEM)] * 2,
        compiler_params=pltpu.CompilerParams(vmem_limit_bytes=8 << 20),
        cost_estimate=pl.CostEstimate(flops=0, bytes_accessed=1 << 20, transcendentals=0),
        name="corners",
    )(left, right, after)


def stencil_parts(weight, a, b, force, n, coef, inv):
    wide, lanes = coef.shape[-2:]
    tiles = wide // TILE

    def over(step, spans):
        for first, end in spans:
            unroll = 3 if (end - first) % 3 == 0 else 2 if (end - first) % 2 == 0 else end - first

            def body(at, _):
                step(at)
                return 0

            lax.fori_loop(first, end, body, 0, unroll=unroll)

    def part(ref, at, t, shift=0):
        return ref[(*at, pl.ds(TILE * (t + 1) + shift, TILE))]

    def put(ref, at, t, value):
        ref[(*at, pl.ds(TILE * (t + 1), TILE))] = value

    def put_round(ref, at, t, value):
        put(ref, at, t, value)
        if t == 0:
            put(ref, at, tiles, value)
        if t == tiles - 1:
            put(ref, at, -1, value)

    def ahead(x):
        return pltpu.roll(x, lanes - 1, 1)

    def behind(x):
        return pltpu.roll(x, 1, 1)

    def lay(ref, at, main):
        for t in range(tiles - 1):
            put_round(ref, at, t, main(t))

    def lay_side(ref, at, side):
        put_round(ref, at, tiles - 1, side)

    def lay_force(c, at, main):
        for t in range(tiles - 1):
            force[c, at, pl.ds(TILE * t, TILE)] = main(t)

    def lay_force_side(c, at, side):
        force[c, at, pl.ds(TILE * (tiles - 1), TILE)] = side

    def of(ref, *at):
        return lambda t: ref[(*at, pl.ds(TILE * t, TILE))]

    def total(terms):
        while len(terms) > 1:
            terms = [sum(terms[i : i + 2]) for i in range(0, len(terms), 2)]
        return terms[0]

    def coef_row(at, chosen):
        for t in chosen:
            here = part(n, (at,), t)
            sums, j = [], 0
            for group, own in zip(GROUPS, (here, behind(here), ahead(here))):
                cs = []
                for up, side, _ in group:
                    cs.append(weight[j] * (own + part(n, (at + up,), t, side)))
                    coef[j, at, pl.ds(TILE * t, TILE)] = cs[-1]
                    j += 1
                sums.append(total(cs))
            diag = (sums[0] + weight[NEAR] * here) + (ahead(sums[1]) + behind(sums[2]))
            inv[at, pl.ds(TILE * t, TILE)] = jnp.where(here > 0.0, 1.0 / diag, 0.0)

    def coefs(spans, chosen=range(tiles)):
        over(lambda at: coef_row(at, chosen), spans)

    def sweep(field, store, spans, chosen=range(tiles)):
        def step(at):
            for t in chosen:
                here = pl.ds(TILE * t, TILE)
                cs = [coef[j, at, here] for j in range(NEAR)]
                invd = inv[at, here]
                for c in range(COMP):
                    sums, j = [], 0
                    for group in GROUPS:
                        terms = []
                        for up, side, _ in group:
                            terms.append(cs[j] * part(field, (c, at + up), t, side))
                            j += 1
                        sums.append(total(terms))
                    target = (sums[0] + force[c, at, here]) + (ahead(sums[1]) + behind(sums[2]))
                    store(c, at, t, part(field, (c, at), t), target * invd)

        over(step, spans)

    def store1(c, at, t, v, target):
        put_round(b, (c, at), t, (1.0 - OMEGA) * v + OMEGA * target)

    def store2(c, at, t, v, target):
        put_round(a, (c, at), t, (1.0 - OMEGA) * v + OMEGA * target)

    def store3(c, at, t, v, target):
        b[c, at, pl.ds(TILE * (t + 1), TILE)] = target - v

    return (
        (lay, lay_side, lay_force, lay_force_side, of),
        coefs,
        functools.partial(sweep, a, store1),
        functools.partial(sweep, b, store2),
        functools.partial(sweep, a, store3),
    )


def middle_kernel(weight, u, rhs, visc, a, b, force, n, coef, inv):
    rows, cols, _ = visc.shape
    laying, coefs, sweep1, sweep2, residual = stencil_parts(weight, a, b, force, n, coef, inv)
    lay, _, lay_force, _, of = laying

    def own_step(r, _):
        at = r + BELOW
        for c in range(COMP):
            lay(a, (c, at), of(u, c, r))
            lay_force(c, at, of(rhs, c, r))
        lay(n, (at,), of(visc, r))
        return 0

    first, end, last = BELOW, BELOW + rows, cols // TILE
    lax.fori_loop(0, rows, own_step, 0)
    coefs([(first + 1, end - 1)], range(1, last - 1))
    sweep1([(first + 1, end - 1)], range(1, last - 1))
    sweep2([(first + 2, end - 2)], range(2, last - 2))
    residual([(first + 3, end - 3)], range(3, last - 3))


def inner_kernel(weight, left, right, _, *refs):
    a, b, force, n, coef, inv = refs[6:]
    rows, lanes = 2 * left.shape[1], left.shape[3]
    late = lax.broadcasted_iota(jnp.int32, (TILE, lanes), 0) >= TILE - BELOW
    laying, coefs, sweep1, sweep2, residual = stencil_parts(weight, a, b, force, n, coef, inv)
    _, lay_side, _, lay_force_side, _ = laying

    def own_step(i, _):
        for odd in range(2):
            at = 2 * i + odd + BELOW

            def side(field):
                return jnp.where(late, row_of(left, field, i, odd), row_of(right, field, i, odd))

            for c in range(COMP):
                lay_side(a, (c, at), side(c))
                lay_force_side(c, at, side(COMP + c))
            lay_side(n, (at,), side(2 * COMP))
        return 0

    first, end, last = BELOW, BELOW + rows, inv.shape[1] // TILE - 1

    lax.fori_loop(0, rows // 2, own_step, 0)
    coefs([(first + 1, end - 1)], rest(last, 1))
    sweep1([(first + 1, end - 1)], rest(last, 1))
    sweep2([(first + 2, end - 2)], rest(last, 2))
    residual([(first + 3, end - 3)], rest(last, 3))


def rest(last, edge):
    return [t for t in range(last + 1) if not edge <= t < last - edge]


def halo_rows(rows):
    return ((ABOVE, BELOW + rows, BELOW + rows), (BELOW, 0, 1))


def outer_middle_kernel(weight, above, below, *refs):
    a, b, force, n, coef, inv = refs[6:]
    rows, cols = a.shape[1] - BELOW - ABOVE, above.shape[1]
    laying, coefs, sweep1, sweep2, residual = stencil_parts(weight, a, b, force, n, coef, inv)
    lay, _, lay_force, _, of = laying
    for main, (count, at, at_r) in zip((above, below), halo_rows(rows)):

        def step(i, _):
            for c in range(COMP):
                lay(a, (c, at + i), of(main, c * count + i))
            lay(n, (at + i,), of(main, COMP * count + i))
            return 0

        def step_r(i, _):
            for c in range(COMP):
                lay_force(c, at_r + i, of(main, (COMP + 1) * count + c * (count - 1) + i))
            return 0

        lax.fori_loop(0, count, step, 0)
        lax.fori_loop(0, count - 1, step_r, 0)

    first, end, last = BELOW, BELOW + rows, cols // TILE
    coefs([(first - 2, first + 1), (end - 1, end + 3)], range(1, last - 1))
    sweep1([(first - 2, first + 1), (end - 1, end + 3)], range(1, last - 1))
    sweep2([(first - 1, first + 2), (end - 2, end + 2)], range(2, last - 2))
    residual([(first, first + 3), (end - 3, end + 1)], range(3, last - 3))


def outer_kernel(weight, above_c, below_c, *refs):
    a, b, force, n, coef, inv = refs[6:12]
    smoothed, coarse, restr, sems = refs[12:]
    rows, cols, lanes = smoothed.shape[1:]
    laying, coefs, sweep1, sweep2, residual = stencil_parts(weight, a, b, force, n, coef, inv)
    _, lay_side, _, lay_force_side, _ = laying
    for side, (count, at, at_r) in zip((above_c, below_c), halo_rows(rows)):
        for i in range(count):
            for c in range(COMP):
                lay_side(a, (c, at + i), side[c * count + i])
            lay_side(n, (at + i,), side[COMP * count + i])
        for i in range(count - 1):
            for c in range(COMP):
                lay_force_side(c, at_r + i, side[(COMP + 1) * count + c * (count - 1) + i])

    first, end, last = BELOW, BELOW + rows, cols // TILE
    coefs([(first - 2, first + 1), (end - 1, end + 3)], rest(last, 1))
    sweep1([(first - 2, first + 1), (end - 1, end + 3)], rest(last, 1))
    sweep2([(first - 1, first + 2), (end - 2, end + 2)], rest(last, 2))
    copies = [
        pltpu.make_async_copy(a.at[c, pl.ds(first, rows), pl.ds(TILE, cols)], smoothed.at[c], sems.at[c])
        for c in range(COMP)
    ]
    for each in copies:
        each.start()
    residual([(first, first + 3), (end - 3, end + 1)], rest(last, 3))

    for c in range(COMP):
        for i in range(rows // 2):
            at = BELOW + 2 * i
            restr[c * (rows // 2) + i] = 0.25 * (b[c, at, TILE:] + b[c, at + 2, TILE:]) + 0.5 * b[c, at + 1, TILE:]
    parts = []
    for i in range(COMP * (rows // 2)):
        p = restr[i, pl.ds(0, cols // 2, stride=2)]
        q = restr[i, pl.ds(1, cols // 2, stride=2)]
        d = restr[i, pl.ds(2, cols // 2, stride=2)]
        parts.append(0.25 * (p + d) + 0.5 * q)
    source = lax.broadcasted_iota(jnp.int32, (lanes, lanes // 2), 0)
    target = 2 * lax.broadcasted_iota(jnp.int32, (lanes, lanes // 2), 1)
    gap = source - target
    h = jnp.where(gap == 1, 0.5, jnp.where((gap == 0) | (gap == 2), 0.25, 0.0))
    for c in range(COMP):
        block = jnp.concatenate(parts[c * (rows // 2) : (c + 1) * (rows // 2)], 0)
        out = jnp.dot(block, h, precision=lax.Precision.HIGHEST, preferred_element_type=jnp.float32)
        coarse[c] = out.reshape(rows // 2, cols // 2, lanes // 2)
    for each in copies:
        each.wait()


def state_shapes(rows, cols, lanes):
    deep, wide = rows + BELOW + ABOVE, cols + TILE
    padded = wide + 2 * TILE
    shapes = (
        (COMP, deep, padded, lanes),
        (COMP, deep, padded, lanes),
        (COMP, deep, wide, lanes),
        (deep, padded, lanes),
        (14, deep, wide, lanes),
        (deep, wide, lanes),
    )
    return [jax.ShapeDtypeStruct(s, jnp.float32) for s in shapes]


def middle(weight, u, rhs, visc):
    vmem = pl.BlockSpec(memory_space=pltpu.VMEM)
    return pl.pallas_call(
        middle_kernel,
        out_shape=state_shapes(*visc.shape),
        in_specs=[vmem] * 4,
        out_specs=[vmem] * 6,
        compiler_params=pltpu.CompilerParams(vmem_limit_bytes=16 << 20),
        cost_estimate=pl.CostEstimate(flops=10_000_000, bytes_accessed=8 << 20, transcendentals=0),
        name="middle",
    )(weight, u, rhs, visc)


def inner(weight, left, right, after, state):
    vmem = pl.BlockSpec(memory_space=pltpu.VMEM)
    return pl.pallas_call(
        inner_kernel,
        out_shape=[jax.ShapeDtypeStruct(x.shape, x.dtype) for x in state],
        in_specs=[vmem] * 3 + [pl.BlockSpec(memory_space=pl.ANY)] + [vmem] * 6,
        out_specs=[vmem] * 6,
        input_output_aliases={4 + i: i for i in range(6)},
        compiler_params=pltpu.CompilerParams(vmem_limit_bytes=16 << 20),
        cost_estimate=pl.CostEstimate(flops=10_000_000, bytes_accessed=8 << 20, transcendentals=0),
        name="inner",
    )(weight, left, right, after, *state)


def outer_middle(weight, above, below, state):
    vmem = pl.BlockSpec(memory_space=pltpu.VMEM)
    return pl.pallas_call(
        outer_middle_kernel,
        out_shape=[jax.ShapeDtypeStruct(x.shape, x.dtype) for x in state],
        in_specs=[vmem] * 9,
        out_specs=[vmem] * 6,
        input_output_aliases={3 + i: i for i in range(6)},
        compiler_params=pltpu.CompilerParams(vmem_limit_bytes=16 << 20),
        cost_estimate=pl.CostEstimate(flops=10_000_000, bytes_accessed=8 << 20, transcendentals=0),
        name="outer_middle",
    )(weight, above, below, *state)


def outer(weight, above_c, below_c, state, rows, cols, lanes):
    vmem = pl.BlockSpec(memory_space=pltpu.VMEM)
    f32 = jnp.float32
    shapes = state_shapes(rows, cols, lanes)
    out = pl.pallas_call(
        outer_kernel,
        out_shape=shapes
        + [
            jax.ShapeDtypeStruct((COMP, rows, cols, lanes), f32),
            jax.ShapeDtypeStruct((COMP, rows // 2, cols // 2, lanes // 2), f32),
        ],
        in_specs=[vmem] * 9,
        out_specs=[vmem] * 6 + [pl.BlockSpec(memory_space=pltpu.HBM), vmem],
        input_output_aliases={3 + i: i for i in range(6)},
        scratch_shapes=[
            pltpu.VMEM((COMP * (rows // 2), cols + 2 * TILE, lanes), f32),
            pltpu.SemaphoreType.DMA((COMP,)),
        ],
        compiler_params=pltpu.CompilerParams(vmem_limit_bytes=16 << 20),
        cost_estimate=pl.CostEstimate(flops=20_000_000, bytes_accessed=16 << 20, transcendentals=0),
        name="outer",
    )(weight, above_c, below_c, *state)
    return out[6], out[7]


def sent(value, axis, steps):
    count = lax.axis_size(axis)
    pairs = [(i, i + steps) for i in range(count) if 0 <= i + steps < count]
    return lax.ppermute(value, axis, pairs)


def per_device(solution, right_side, viscosity, stencil_weights):
    to_left, to_right, to_below, to_above, own_visc, weight = pack(stencil_weights, solution, right_side, viscosity)
    above = sent(to_below, "shell", -1)
    below = sent(to_above, "shell", 1)
    left = sent(to_right, "lat", 1)
    right = sent(to_left, "lat", -1)
    state = middle(weight, solution, right_side, own_visc)
    to_below_c, to_above_c = corners(left, right, state[-1])
    above_c = sent(to_below_c, "shell", -1)
    below_c = sent(to_above_c, "shell", 1)
    state = inner(weight, left, right, to_below_c, state)
    state = outer_middle(weight, above, below, state)
    return outer(weight, above_c, below_c, state, *viscosity.shape)


def solution(mesh):
    in_specs = (
        P(None, "shell", "lat", None),
        P(None, "shell", "lat", None),
        P("shell", "lat", None),
        P(),
    )
    out_specs = (P(None, "shell", "lat", None), P(None, "shell", "lat", None))
    return jax.shard_map(
        per_device, mesh=mesh, in_specs=in_specs, out_specs=out_specs, check_vma=False
    )
```

```python
import functools

import jax
import jax.numpy as jnp
from jax import lax
from jax.experimental import pallas as pl
from jax.experimental.pallas import tpu as pltpu
from jax.sharding import PartitionSpec as P

OMEGA = 0.6
COMP = 3
BELOW = 3
LONGEST = 21
ABOVE = 4
TILE = 8


GROUPS = (
    ((1, 0, 0), (0, 1, 1), (1, 1, 3), (-1, 0, 0), (0, -1, 1), (-1, -1, 3)),
    ((0, 0, 2), (1, 0, 4), (0, 1, 5), (1, 1, 6)),
    ((0, 0, 2), (-1, 0, 4), (0, -1, 5), (-1, -1, 6)),
)


def turned(x):
    return pltpu.roll(x, TILE // 2, 0)


def row_of(ref, field, pair, odd):
    return turned(ref[field, pair]) if odd else ref[field, pair]


NEAR = 14


def pack_kernel(
    wts, u, rhs, visc, to_left, to_right, to_below, to_above, own_visc, weight, first_cols, last_cols, held, sems
):
    rows, cols, lanes = visc.shape
    pairs = []
    for buffer, first in ((first_cols, 0), (last_cols, cols - TILE)):
        pairs.append((u.at[:, :, pl.ds(first, TILE)], buffer.at[pl.ds(0, COMP)]))
        pairs.append((rhs.at[:, :, pl.ds(first, TILE)], buffer.at[pl.ds(COMP, COMP)]))
        pairs.append((visc.at[:, pl.ds(first, TILE)], buffer.at[2 * COMP]))
    for buffer, count, first in ((to_below, ABOVE, 0), (to_above, BELOW, rows - BELOW)):
        short, first_r = count - 1, first if first == 0 else first + 1
        for c in range(COMP):
            pairs.append((u.at[c, pl.ds(first, count)], buffer.at[pl.ds(c * count, count)]))
        pairs.append((visc.at[pl.ds(first, count)], buffer.at[pl.ds(COMP * count, count)]))
        for c in range(COMP):
            at = (COMP + 1) * count + c * short
            pairs.append((rhs.at[c, pl.ds(first_r, short)], buffer.at[pl.ds(at, short)]))
    pairs.append((wts, held))
    pairs.append((visc, own_visc))
    copies = [pltpu.make_async_copy(src, dst, sems.at[i]) for i, (src, dst) in enumerate(pairs)]
    for each in copies:
        each.start()
    for each in copies[:6]:
        each.wait()
    low = lax.broadcasted_iota(jnp.int32, (TILE, lanes), 0) < TILE // 2
    for field in range(2 * COMP + 1):
        for i in range(rows // 2):
            a, b = first_cols[field, 2 * i], first_cols[field, 2 * i + 1]
            to_left[field, i] = jnp.where(low, a, turned(b))
            a, b = last_cols[field, 2 * i], last_cols[field, 2 * i + 1]
            to_right[field, i] = jnp.where(low, turned(b), a)
    for each in copies[6:]:
        each.wait()
    lane = lax.broadcasted_iota(jnp.int32, (TILE, lanes), 1)
    half = [0.5 * held[k] for k in range(7)]
    j = 0
    for group, inside in zip(GROUPS, (lane >= 0, lane > 0, lane < lanes - 1)):
        for _, _, k in group:
            weight[j] = jnp.where(inside, half[k], 0.0)
            j += 1
    lost = half[2] + half[4] + half[5] + half[6]
    weight[j] = jnp.where((lane == 0) | (lane == lanes - 1), lost, 0.0)


def shell_rows(count):
    return (COMP + 1) * count + COMP * (count - 1)


def pack(wts, u, rhs, visc):
    rows, cols, lanes = visc.shape
    shapes = ((2 * COMP + 1, rows // 2, TILE, lanes),) * 2
    shapes += ((shell_rows(ABOVE), cols, lanes), (shell_rows(BELOW), cols, lanes))
    shapes += (visc.shape, (NEAR + 1, TILE, lanes))
    return pl.pallas_call(
        pack_kernel,
        out_shape=[jax.ShapeDtypeStruct(s, jnp.float32) for s in shapes],
        in_specs=[pl.BlockSpec(memory_space=pltpu.HBM)] * 4,
        out_specs=[pl.BlockSpec(memory_space=pltpu.VMEM)] * 6,
        scratch_shapes=[pltpu.VMEM((2 * COMP + 1, rows, TILE, lanes), jnp.float32)] * 2
        + [pltpu.SMEM((7,), jnp.float32), pltpu.SemaphoreType.DMA((22,))],
        compiler_params=pltpu.CompilerParams(vmem_limit_bytes=8 << 20),
        cost_estimate=pl.CostEstimate(flops=0, bytes_accessed=4 << 20, transcendentals=0),
        name="pack",
    )(*(pltpu.with_memory_space_constraint(x, pltpu.HBM) for x in (wts, u, rhs, visc)))


def corner_kernel(left, right, _, to_below, to_above):
    rows = 2 * left.shape[1]
    late = lax.broadcasted_iota(jnp.int32, left.shape[2:], 0) >= TILE - BELOW

    def rows_of(buffer, count, first_n, first_r, count_r):
        at = 0
        picks = [(c, first_n + i) for c in range(COMP) for i in range(count)]
        picks += [(2 * COMP, first_n + i) for i in range(count)]
        picks += [(COMP + c, first_r + i) for c in range(COMP) for i in range(count_r)]
        for field, row in picks:
            buffer[at] = jnp.where(
                late, row_of(left, field, row // 2, row % 2), row_of(right, field, row // 2, row % 2)
            )
            at += 1

    rows_of(to_below, ABOVE, 0, 0, ABOVE - 1)
    rows_of(to_above, BELOW, rows - BELOW, rows - BELOW + 1, BELOW - 1)


def corners(left, right, after):
    lanes = left.shape[-1]
    shapes = (
        ((4 * ABOVE + 3 * (ABOVE - 1)), TILE, lanes),
        ((4 * BELOW + 3 * (BELOW - 1)), TILE, lanes),
    )
    return pl.pallas_call(
        corner_kernel,
        out_shape=[jax.ShapeDtypeStruct(s, jnp.float32) for s in shapes],
        in_specs=[pl.BlockSpec(memory_space=pltpu.VMEM)] * 2 + [pl.BlockSpec(memory_space=pl.ANY)],
        out_specs=[pl.BlockSpec(memory_space=pltpu.VMEM)] * 2,
        compiler_params=pltpu.CompilerParams(vmem_limit_bytes=8 << 20),
        cost_estimate=pl.CostEstimate(flops=0, bytes_accessed=1 << 20, transcendentals=0),
        name="corners",
    )(left, right, after)


def stencil_parts(weight, a, b, force, n, coef, inv):
    wide, lanes = coef.shape[-2:]
    tiles = wide // TILE

    def over(step, spans, width):
        for first, end in spans:
            unroll = max(u for u in (1, 2, 3, 4, 6) if (end - first) % u == 0 and (u <= 2 or u * width <= LONGEST))

            def body(at, _):
                step(at)
                return 0

            lax.fori_loop(first, end, body, 0, unroll=unroll)

    def part(ref, at, t, shift=0):
        return ref[(*at, pl.ds(TILE * (t + 1) + shift, TILE))]

    def put(ref, at, t, value):
        ref[(*at, pl.ds(TILE * (t + 1), TILE))] = value

    def put_round(ref, at, t, value):
        put(ref, at, t, value)
        if t == 0:
            put(ref, at, tiles, value)
        if t == tiles - 1:
            put(ref, at, -1, value)

    def ahead(x):
        return pltpu.roll(x, lanes - 1, 1)

    def behind(x):
        return pltpu.roll(x, 1, 1)

    def lay(ref, at, main):
        for t in range(tiles - 1):
            put_round(ref, at, t, main(t))

    def lay_side(ref, at, side):
        put_round(ref, at, tiles - 1, side)

    def lay_force(c, at, main):
        for t in range(tiles - 1):
            force[c, at, pl.ds(TILE * t, TILE)] = main(t)

    def lay_force_side(c, at, side):
        force[c, at, pl.ds(TILE * (tiles - 1), TILE)] = side

    def of(ref, *at):
        return lambda t: ref[(*at, pl.ds(TILE * t, TILE))]

    def total(terms):
        while len(terms) > 1:
            terms = [sum(terms[i : i + 2]) for i in range(0, len(terms), 2)]
        return terms[0]

    def coef_row(at, chosen):
        for t in chosen:
            here = part(n, (at,), t)
            sums, j = [], 0
            for group, own in zip(GROUPS, (here, behind(here), ahead(here))):
                cs = []
                for up, side, _ in group:
                    cs.append(weight[j] * (own + part(n, (at + up,), t, side)))
                    coef[j, at, pl.ds(TILE * t, TILE)] = cs[-1]
                    j += 1
                sums.append(total(cs))
            diag = (sums[0] + weight[NEAR] * here) + (ahead(sums[1]) + behind(sums[2]))
            inv[at, pl.ds(TILE * t, TILE)] = jnp.where(here > 0.0, OMEGA / diag, 0.0)

    def coefs(spans, chosen=range(tiles)):
        over(lambda at: coef_row(at, chosen), spans, len(chosen))

    def sweep(field, store, spans, chosen=range(tiles)):
        def step(at):
            for t in chosen:
                here = pl.ds(TILE * t, TILE)
                cs = [coef[j, at, here] for j in range(NEAR)]
                invd = inv[at, here]
                for c in range(COMP):
                    sums, j = [], 0
                    for group in GROUPS:
                        terms = []
                        for up, side, _ in group:
                            terms.append(cs[j] * part(field, (c, at + up), t, side))
                            j += 1
                        sums.append(total(terms))
                    target = (sums[0] + force[c, at, here]) + (ahead(sums[1]) + behind(sums[2]))
                    store(c, at, t, part(field, (c, at), t), target * invd)

        over(step, spans, len(chosen))

    def store1(c, at, t, v, target):
        put_round(b, (c, at), t, (1.0 - OMEGA) * v + target)

    def store2(c, at, t, v, target):
        put_round(a, (c, at), t, (1.0 - OMEGA) * v + target)

    def store3(c, at, t, v, target):
        b[c, at, pl.ds(TILE * (t + 1), TILE)] = (1.0 / OMEGA) * target - v

    return (
        (lay, lay_side, lay_force, lay_force_side, of),
        coefs,
        functools.partial(sweep, a, store1),
        functools.partial(sweep, b, store2),
        functools.partial(sweep, a, store3),
    )


def middle_kernel(weight, u, rhs, visc, a, b, force, n, coef, inv):
    rows, cols, _ = visc.shape
    laying, coefs, sweep1, sweep2, residual = stencil_parts(weight, a, b, force, n, coef, inv)
    lay, _, lay_force, _, of = laying

    def own_step(r, _):
        at = r + BELOW
        for c in range(COMP):
            lay(a, (c, at), of(u, c, r))
            lay_force(c, at, of(rhs, c, r))
        lay(n, (at,), of(visc, r))
        return 0

    first, end, last = BELOW, BELOW + rows, cols // TILE
    lax.fori_loop(0, rows, own_step, 0)
    coefs([(first + 1, end - 1)], range(1, last - 1))
    sweep1([(first + 1, end - 1)], range(1, last - 1))
    sweep2([(first + 2, end - 2)], range(2, last - 2))
    residual([(first + 3, end - 3)], range(3, last - 3))


def inner_kernel(weight, left, right, _, *refs):
    a, b, force, n, coef, inv = refs[6:]
    rows, lanes = 2 * left.shape[1], left.shape[3]
    late = lax.broadcasted_iota(jnp.int32, (TILE, lanes), 0) >= TILE - BELOW
    laying, coefs, sweep1, sweep2, residual = stencil_parts(weight, a, b, force, n, coef, inv)
    _, lay_side, _, lay_force_side, _ = laying

    def own_step(i, _):
        for odd in range(2):
            at = 2 * i + odd + BELOW

            def side(field):
                return jnp.where(late, row_of(left, field, i, odd), row_of(right, field, i, odd))

            for c in range(COMP):
                lay_side(a, (c, at), side(c))
                lay_force_side(c, at, side(COMP + c))
            lay_side(n, (at,), side(2 * COMP))
        return 0

    first, end, last = BELOW, BELOW + rows, inv.shape[1] // TILE - 1

    lax.fori_loop(0, rows // 2, own_step, 0)
    coefs([(first + 1, end - 1)], rest(last, 1))
    sweep1([(first + 1, end - 1)], rest(last, 1))
    sweep2([(first + 2, end - 2)], rest(last, 2))
    residual([(first + 3, end - 3)], rest(last, 3))


def rest(last, edge):
    return [t for t in range(last + 1) if not edge <= t < last - edge]


def halo_rows(rows):
    return ((ABOVE, BELOW + rows, BELOW + rows), (BELOW, 0, 1))


def outer_middle_kernel(weight, above, below, *refs):
    a, b, force, n, coef, inv = refs[6:]
    rows, cols = a.shape[1] - BELOW - ABOVE, above.shape[1]
    laying, coefs, sweep1, sweep2, residual = stencil_parts(weight, a, b, force, n, coef, inv)
    lay, _, lay_force, _, of = laying
    for main, (count, at, at_r) in zip((above, below), halo_rows(rows)):

        def step(i, _):
            for c in range(COMP):
                lay(a, (c, at + i), of(main, c * count + i))
            lay(n, (at + i,), of(main, COMP * count + i))
            return 0

        def step_r(i, _):
            for c in range(COMP):
                lay_force(c, at_r + i, of(main, (COMP + 1) * count + c * (count - 1) + i))
            return 0

        lax.fori_loop(0, count, step, 0)
        lax.fori_loop(0, count - 1, step_r, 0)

    first, end, last = BELOW, BELOW + rows, cols // TILE
    coefs([(first - 2, first + 1), (end - 1, end + 3)], range(1, last - 1))
    sweep1([(first - 2, first + 1), (end - 1, end + 3)], range(1, last - 1))
    sweep2([(first - 1, first + 2), (end - 2, end + 2)], range(2, last - 2))
    residual([(first, first + 3), (end - 3, end + 1)], range(3, last - 3))


def outer_kernel(weight, above_c, below_c, *refs):
    a, b, force, n, coef, inv = refs[6:12]
    smoothed, coarse, restr, sems = refs[12:]
    rows, cols, lanes = smoothed.shape[1:]
    laying, coefs, sweep1, sweep2, residual = stencil_parts(weight, a, b, force, n, coef, inv)
    _, lay_side, _, lay_force_side, _ = laying
    for side, (count, at, at_r) in zip((above_c, below_c), halo_rows(rows)):
        for i in range(count):
            for c in range(COMP):
                lay_side(a, (c, at + i), side[c * count + i])
            lay_side(n, (at + i,), side[COMP * count + i])
        for i in range(count - 1):
            for c in range(COMP):
                lay_force_side(c, at_r + i, side[(COMP + 1) * count + c * (count - 1) + i])

    first, end, last = BELOW, BELOW + rows, cols // TILE
    coefs([(first - 2, first + 1), (end - 1, end + 3)], rest(last, 1))
    sweep1([(first - 2, first + 1), (end - 1, end + 3)], rest(last, 1))
    sweep2([(first - 1, first + 2), (end - 2, end + 2)], rest(last, 2))
    copies = [
        pltpu.make_async_copy(a.at[c, pl.ds(first, rows), pl.ds(TILE, cols)], smoothed.at[c], sems.at[c])
        for c in range(COMP)
    ]
    for each in copies:
        each.start()
    residual([(first, first + 3), (end - 3, end + 1)], rest(last, 3))

    for c in range(COMP):
        for i in range(rows // 2):
            at = BELOW + 2 * i
            restr[c * (rows // 2) + i] = 0.25 * (b[c, at, TILE:] + b[c, at + 2, TILE:]) + 0.5 * b[c, at + 1, TILE:]
    parts = []
    for i in range(COMP * (rows // 2)):
        p = restr[i, pl.ds(0, cols // 2, stride=2)]
        q = restr[i, pl.ds(1, cols // 2, stride=2)]
        d = restr[i, pl.ds(2, cols // 2, stride=2)]
        parts.append(0.25 * (p + d) + 0.5 * q)
    source = lax.broadcasted_iota(jnp.int32, (lanes, lanes // 2), 0)
    target = 2 * lax.broadcasted_iota(jnp.int32, (lanes, lanes // 2), 1)
    gap = source - target
    h = jnp.where(gap == 1, 0.5, jnp.where((gap == 0) | (gap == 2), 0.25, 0.0))
    for c in range(COMP):
        block = jnp.concatenate(parts[c * (rows // 2) : (c + 1) * (rows // 2)], 0)
        out = jnp.dot(block, h, precision=lax.Precision.HIGHEST, preferred_element_type=jnp.float32)
        coarse[c] = out.reshape(rows // 2, cols // 2, lanes // 2)
    for each in copies:
        each.wait()


def state_shapes(rows, cols, lanes):
    deep, wide = rows + BELOW + ABOVE, cols + TILE
    padded = wide + 2 * TILE
    shapes = (
        (COMP, deep, padded, lanes),
        (COMP, deep, padded, lanes),
        (COMP, deep, wide, lanes),
        (deep, padded, lanes),
        (14, deep, wide, lanes),
        (deep, wide, lanes),
    )
    return [jax.ShapeDtypeStruct(s, jnp.float32) for s in shapes]


def middle(weight, u, rhs, visc):
    vmem = pl.BlockSpec(memory_space=pltpu.VMEM)
    return pl.pallas_call(
        middle_kernel,
        out_shape=state_shapes(*visc.shape),
        in_specs=[vmem] * 4,
        out_specs=[vmem] * 6,
        compiler_params=pltpu.CompilerParams(vmem_limit_bytes=16 << 20),
        cost_estimate=pl.CostEstimate(flops=10_000_000, bytes_accessed=8 << 20, transcendentals=0),
        name="middle",
    )(weight, u, rhs, visc)


def inner(weight, left, right, after, state):
    vmem = pl.BlockSpec(memory_space=pltpu.VMEM)
    return pl.pallas_call(
        inner_kernel,
        out_shape=[jax.ShapeDtypeStruct(x.shape, x.dtype) for x in state],
        in_specs=[vmem] * 3 + [pl.BlockSpec(memory_space=pl.ANY)] + [vmem] * 6,
        out_specs=[vmem] * 6,
        input_output_aliases={4 + i: i for i in range(6)},
        compiler_params=pltpu.CompilerParams(vmem_limit_bytes=16 << 20),
        cost_estimate=pl.CostEstimate(flops=10_000_000, bytes_accessed=8 << 20, transcendentals=0),
        name="inner",
    )(weight, left, right, after, *state)


def outer_middle(weight, above, below, state):
    vmem = pl.BlockSpec(memory_space=pltpu.VMEM)
    return pl.pallas_call(
        outer_middle_kernel,
        out_shape=[jax.ShapeDtypeStruct(x.shape, x.dtype) for x in state],
        in_specs=[vmem] * 9,
        out_specs=[vmem] * 6,
        input_output_aliases={3 + i: i for i in range(6)},
        compiler_params=pltpu.CompilerParams(vmem_limit_bytes=16 << 20),
        cost_estimate=pl.CostEstimate(flops=10_000_000, bytes_accessed=8 << 20, transcendentals=0),
        name="outer_middle",
    )(weight, above, below, *state)


def outer(weight, above_c, below_c, state, rows, cols, lanes):
    vmem = pl.BlockSpec(memory_space=pltpu.VMEM)
    f32 = jnp.float32
    shapes = state_shapes(rows, cols, lanes)
    out = pl.pallas_call(
        outer_kernel,
        out_shape=shapes
        + [
            jax.ShapeDtypeStruct((COMP, rows, cols, lanes), f32),
            jax.ShapeDtypeStruct((COMP, rows // 2, cols // 2, lanes // 2), f32),
        ],
        in_specs=[vmem] * 9,
        out_specs=[vmem] * 6 + [pl.BlockSpec(memory_space=pltpu.HBM), vmem],
        input_output_aliases={3 + i: i for i in range(6)},
        scratch_shapes=[
            pltpu.VMEM((COMP * (rows // 2), cols + 2 * TILE, lanes), f32),
            pltpu.SemaphoreType.DMA((COMP,)),
        ],
        compiler_params=pltpu.CompilerParams(vmem_limit_bytes=16 << 20),
        cost_estimate=pl.CostEstimate(flops=20_000_000, bytes_accessed=16 << 20, transcendentals=0),
        name="outer",
    )(weight, above_c, below_c, *state)
    return out[6], out[7]


def sent(value, axis, steps):
    count = lax.axis_size(axis)
    pairs = [(i, i + steps) for i in range(count) if 0 <= i + steps < count]
    return lax.ppermute(value, axis, pairs)


def per_device(solution, right_side, viscosity, stencil_weights):
    to_left, to_right, to_below, to_above, own_visc, weight = pack(stencil_weights, solution, right_side, viscosity)
    above = sent(to_below, "shell", -1)
    below = sent(to_above, "shell", 1)
    left = sent(to_right, "lat", 1)
    right = sent(to_left, "lat", -1)
    state = middle(weight, solution, right_side, own_visc)
    to_below_c, to_above_c = corners(left, right, state[-1])
    above_c = sent(to_below_c, "shell", -1)
    below_c = sent(to_above_c, "shell", 1)
    state = inner(weight, left, right, to_below_c, state)
    state = outer_middle(weight, above, below, state)
    return outer(weight, above_c, below_c, state, *viscosity.shape)


def solution(mesh):
    in_specs = (
        P(None, "shell", "lat", None),
        P(None, "shell", "lat", None),
        P("shell", "lat", None),
        P(),
    )
    out_specs = (P(None, "shell", "lat", None), P(None, "shell", "lat", None))
    return jax.shard_map(
        per_device, mesh=mesh, in_specs=in_specs, out_specs=out_specs, check_vma=False
    )
```

```python
import functools

import jax
import jax.numpy as jnp
from jax import lax
from jax.experimental import pallas as pl
from jax.experimental.pallas import tpu as pltpu
from jax.sharding import PartitionSpec as P

OMEGA = 0.6
COMP = 3
BELOW = 3
LONGEST = 21
ABOVE = 4
TILE = 8


GROUPS = (
    ((1, 0, 0), (0, 1, 1), (1, 1, 3), (-1, 0, 0), (0, -1, 1), (-1, -1, 3)),
    ((0, 0, 2), (1, 0, 4), (0, 1, 5), (1, 1, 6)),
    ((0, 0, 2), (-1, 0, 4), (0, -1, 5), (-1, -1, 6)),
)


def turned(x):
    return pltpu.roll(x, TILE // 2, 0)


def row_of(ref, field, pair, odd):
    return turned(ref[field, pair]) if odd else ref[field, pair]


NEAR = 14


def pack_kernel(
    wts, u, rhs, visc, to_left, to_right, to_below, to_above, own_visc, weight, first_cols, last_cols, held, sems
):
    rows, cols, lanes = visc.shape
    pairs = [(wts, held)]
    for buffer, first in ((first_cols, 0), (last_cols, cols - TILE)):
        pairs.append((u.at[:, :, pl.ds(first, TILE)], buffer.at[pl.ds(0, COMP)]))
        pairs.append((rhs.at[:, :, pl.ds(first, TILE)], buffer.at[pl.ds(COMP, COMP)]))
        pairs.append((visc.at[:, pl.ds(first, TILE)], buffer.at[2 * COMP]))
    for buffer, count, first in ((to_below, ABOVE, 0), (to_above, BELOW, rows - BELOW)):
        short, first_r = count - 1, first if first == 0 else first + 1
        for c in range(COMP):
            pairs.append((u.at[c, pl.ds(first, count)], buffer.at[pl.ds(c * count, count)]))
        pairs.append((visc.at[pl.ds(first, count)], buffer.at[pl.ds(COMP * count, count)]))
        for c in range(COMP):
            at = (COMP + 1) * count + c * short
            pairs.append((rhs.at[c, pl.ds(first_r, short)], buffer.at[pl.ds(at, short)]))
    pairs.append((visc, own_visc))
    copies = [pltpu.make_async_copy(src, dst, sems.at[i]) for i, (src, dst) in enumerate(pairs)]
    for each in copies:
        each.start()
    copies[0].wait()
    lane = lax.broadcasted_iota(jnp.int32, (TILE, lanes), 1)
    half = [0.5 * held[k] for k in range(7)]
    j = 0
    for group, inside in zip(GROUPS, (lane >= 0, lane > 0, lane < lanes - 1)):
        for _, _, k in group:
            weight[j] = jnp.where(inside, half[k], 0.0)
            j += 1
    lost = half[2] + half[4] + half[5] + half[6]
    weight[j] = jnp.where((lane == 0) | (lane == lanes - 1), lost, 0.0)
    for each in copies[1:7]:
        each.wait()
    low = lax.broadcasted_iota(jnp.int32, (TILE, lanes), 0) < TILE // 2
    for field in range(2 * COMP + 1):
        for i in range(rows // 2):
            a, b = first_cols[field, 2 * i], first_cols[field, 2 * i + 1]
            to_left[field, i] = jnp.where(low, a, turned(b))
            a, b = last_cols[field, 2 * i], last_cols[field, 2 * i + 1]
            to_right[field, i] = jnp.where(low, turned(b), a)
    for each in copies[7:]:
        each.wait()


def shell_rows(count):
    return (COMP + 1) * count + COMP * (count - 1)


def pack(wts, u, rhs, visc):
    rows, cols, lanes = visc.shape
    shapes = ((2 * COMP + 1, rows // 2, TILE, lanes),) * 2
    shapes += ((shell_rows(ABOVE), cols, lanes), (shell_rows(BELOW), cols, lanes))
    shapes += (visc.shape, (NEAR + 1, TILE, lanes))
    return pl.pallas_call(
        pack_kernel,
        out_shape=[jax.ShapeDtypeStruct(s, jnp.float32) for s in shapes],
        in_specs=[pl.BlockSpec(memory_space=pltpu.HBM)] * 4,
        out_specs=[pl.BlockSpec(memory_space=pltpu.VMEM)] * 6,
        scratch_shapes=[pltpu.VMEM((2 * COMP + 1, rows, TILE, lanes), jnp.float32)] * 2
        + [pltpu.SMEM((7,), jnp.float32), pltpu.SemaphoreType.DMA((22,))],
        compiler_params=pltpu.CompilerParams(vmem_limit_bytes=8 << 20),
        cost_estimate=pl.CostEstimate(flops=0, bytes_accessed=4 << 20, transcendentals=0),
        name="pack",
    )(*(pltpu.with_memory_space_constraint(x, pltpu.HBM) for x in (wts, u, rhs, visc)))


def corner_kernel(left, right, _, to_below, to_above):
    rows = 2 * left.shape[1]
    late = lax.broadcasted_iota(jnp.int32, left.shape[2:], 0) >= TILE - BELOW

    def rows_of(buffer, count, first_n, first_r, count_r):
        at = 0
        picks = [(c, first_n + i) for c in range(COMP) for i in range(count)]
        picks += [(2 * COMP, first_n + i) for i in range(count)]
        picks += [(COMP + c, first_r + i) for c in range(COMP) for i in range(count_r)]
        for field, row in picks:
            buffer[at] = jnp.where(
                late, row_of(left, field, row // 2, row % 2), row_of(right, field, row // 2, row % 2)
            )
            at += 1

    rows_of(to_below, ABOVE, 0, 0, ABOVE - 1)
    rows_of(to_above, BELOW, rows - BELOW, rows - BELOW + 1, BELOW - 1)


def corners(left, right, after):
    lanes = left.shape[-1]
    shapes = (
        ((4 * ABOVE + 3 * (ABOVE - 1)), TILE, lanes),
        ((4 * BELOW + 3 * (BELOW - 1)), TILE, lanes),
    )
    return pl.pallas_call(
        corner_kernel,
        out_shape=[jax.ShapeDtypeStruct(s, jnp.float32) for s in shapes],
        in_specs=[pl.BlockSpec(memory_space=pltpu.VMEM)] * 2 + [pl.BlockSpec(memory_space=pl.ANY)],
        out_specs=[pl.BlockSpec(memory_space=pltpu.VMEM)] * 2,
        compiler_params=pltpu.CompilerParams(vmem_limit_bytes=8 << 20),
        cost_estimate=pl.CostEstimate(flops=0, bytes_accessed=1 << 20, transcendentals=0),
        name="corners",
    )(left, right, after)


def stencil_parts(weight, a, b, force, n, coef, inv):
    wide, lanes = coef.shape[-2:]
    tiles = wide // TILE

    def over(step, spans, width):
        for first, end in spans:
            unroll = max(u for u in (1, 2, 3, 4, 6) if (end - first) % u == 0 and (u <= 2 or u * width <= LONGEST))

            def body(at, _):
                step(at)
                return 0

            lax.fori_loop(first, end, body, 0, unroll=unroll)

    def part(ref, at, t, shift=0):
        return ref[(*at, pl.ds(TILE * (t + 1) + shift, TILE))]

    def put(ref, at, t, value):
        ref[(*at, pl.ds(TILE * (t + 1), TILE))] = value

    def put_round(ref, at, t, value):
        put(ref, at, t, value)
        if t == 0:
            put(ref, at, tiles, value)
        if t == tiles - 1:
            put(ref, at, -1, value)

    def ahead(x):
        return pltpu.roll(x, lanes - 1, 1)

    def behind(x):
        return pltpu.roll(x, 1, 1)

    def lay(ref, at, main):
        for t in range(tiles - 1):
            put_round(ref, at, t, main(t))

    def lay_side(ref, at, side):
        put_round(ref, at, tiles - 1, side)

    def lay_force(c, at, main):
        for t in range(tiles - 1):
            force[c, at, pl.ds(TILE * t, TILE)] = main(t)

    def lay_force_side(c, at, side):
        force[c, at, pl.ds(TILE * (tiles - 1), TILE)] = side

    def of(ref, *at):
        return lambda t: ref[(*at, pl.ds(TILE * t, TILE))]

    def total(terms):
        while len(terms) > 1:
            terms = [sum(terms[i : i + 2]) for i in range(0, len(terms), 2)]
        return terms[0]

    def coef_row(at, chosen):
        for t in chosen:
            here = part(n, (at,), t)
            sums, j = [], 0
            for group, own in zip(GROUPS, (here, behind(here), ahead(here))):
                cs = []
                for up, side, _ in group:
                    cs.append(weight[j] * (own + part(n, (at + up,), t, side)))
                    coef[j, at, pl.ds(TILE * t, TILE)] = cs[-1]
                    j += 1
                sums.append(total(cs))
            diag = (sums[0] + weight[NEAR] * here) + (ahead(sums[1]) + behind(sums[2]))
            inv[at, pl.ds(TILE * t, TILE)] = jnp.where(here > 0.0, OMEGA / diag, 0.0)

    def coefs(spans, chosen=range(tiles)):
        over(lambda at: coef_row(at, chosen), spans, len(chosen))

    def sweep(field, store, spans, chosen=range(tiles)):
        def step(at):
            for t in chosen:
                here = pl.ds(TILE * t, TILE)
                cs = [coef[j, at, here] for j in range(NEAR)]
                invd = inv[at, here]
                for c in range(COMP):
                    sums, j = [], 0
                    for group in GROUPS:
                        terms = []
                        for up, side, _ in group:
                            terms.append(cs[j] * part(field, (c, at + up), t, side))
                            j += 1
                        sums.append(total(terms))
                    target = (sums[0] + force[c, at, here]) + (ahead(sums[1]) + behind(sums[2]))
                    store(c, at, t, part(field, (c, at), t), target * invd)

        over(step, spans, len(chosen))

    def store1(c, at, t, v, target):
        put_round(b, (c, at), t, (1.0 - OMEGA) * v + target)

    def store2(c, at, t, v, target):
        put_round(a, (c, at), t, (1.0 - OMEGA) * v + target)

    def store3(c, at, t, v, target):
        b[c, at, pl.ds(TILE * (t + 1), TILE)] = (1.0 / OMEGA) * target - v

    return (
        (lay, lay_side, lay_force, lay_force_side, of),
        coefs,
        functools.partial(sweep, a, store1),
        functools.partial(sweep, b, store2),
        functools.partial(sweep, a, store3),
    )


def middle_kernel(weight, u, rhs, visc, a, b, force, n, coef, inv):
    rows, cols, _ = visc.shape
    laying, coefs, sweep1, sweep2, residual = stencil_parts(weight, a, b, force, n, coef, inv)
    lay, _, lay_force, _, of = laying

    def own_step(r, _):
        at = r + BELOW
        for c in range(COMP):
            lay(a, (c, at), of(u, c, r))
            lay_force(c, at, of(rhs, c, r))
        lay(n, (at,), of(visc, r))
        return 0

    first, end, last = BELOW, BELOW + rows, cols // TILE
    lax.fori_loop(0, rows, own_step, 0)
    coefs([(first + 1, end - 1)], range(1, last - 1))
    sweep1([(first + 1, end - 1)], range(1, last - 1))
    sweep2([(first + 2, end - 2)], range(2, last - 2))
    residual([(first + 3, end - 3)], range(3, last - 3))


def inner_kernel(weight, left, right, _, *refs):
    a, b, force, n, coef, inv = refs[6:]
    rows, lanes = 2 * left.shape[1], left.shape[3]
    late = lax.broadcasted_iota(jnp.int32, (TILE, lanes), 0) >= TILE - BELOW
    laying, coefs, sweep1, sweep2, residual = stencil_parts(weight, a, b, force, n, coef, inv)
    _, lay_side, _, lay_force_side, _ = laying

    def own_step(i, _):
        for odd in range(2):
            at = 2 * i + odd + BELOW

            def side(field):
                return jnp.where(late, row_of(left, field, i, odd), row_of(right, field, i, odd))

            for c in range(COMP):
                lay_side(a, (c, at), side(c))
                lay_force_side(c, at, side(COMP + c))
            lay_side(n, (at,), side(2 * COMP))
        return 0

    first, end, last = BELOW, BELOW + rows, inv.shape[1] // TILE - 1

    lax.fori_loop(0, rows // 2, own_step, 0)
    coefs([(first + 1, end - 1)], rest(last, 1))
    sweep1([(first + 1, end - 1)], rest(last, 1))
    sweep2([(first + 2, end - 2)], rest(last, 2))
    residual([(first + 3, end - 3)], rest(last, 3))


def rest(last, edge):
    return [t for t in range(last + 1) if not edge <= t < last - edge]


def halo_rows(rows):
    return ((ABOVE, BELOW + rows, BELOW + rows), (BELOW, 0, 1))


def outer_middle_kernel(weight, above, below, *refs):
    a, b, force, n, coef, inv = refs[6:]
    rows, cols = a.shape[1] - BELOW - ABOVE, above.shape[1]
    laying, coefs, sweep1, sweep2, residual = stencil_parts(weight, a, b, force, n, coef, inv)
    lay, _, lay_force, _, of = laying
    for main, (count, at, at_r) in zip((above, below), halo_rows(rows)):

        def step(i, _):
            for c in range(COMP):
                lay(a, (c, at + i), of(main, c * count + i))
            lay(n, (at + i,), of(main, COMP * count + i))
            return 0

        def step_r(i, _):
            for c in range(COMP):
                lay_force(c, at_r + i, of(main, (COMP + 1) * count + c * (count - 1) + i))
            return 0

        lax.fori_loop(0, count, step, 0)
        lax.fori_loop(0, count - 1, step_r, 0)

    first, end, last = BELOW, BELOW + rows, cols // TILE
    coefs([(first - 2, first + 1), (end - 1, end + 3)], range(1, last - 1))
    sweep1([(first - 2, first + 1), (end - 1, end + 3)], range(1, last - 1))
    sweep2([(first - 1, first + 2), (end - 2, end + 2)], range(2, last - 2))
    residual([(first, first + 3), (end - 3, end + 1)], range(3, last - 3))


def outer_kernel(weight, above_c, below_c, *refs):
    a, b, force, n, coef, inv = refs[6:12]
    smoothed, coarse, restr, sems = refs[12:]
    rows, cols, lanes = smoothed.shape[1:]
    laying, coefs, sweep1, sweep2, residual = stencil_parts(weight, a, b, force, n, coef, inv)
    _, lay_side, _, lay_force_side, _ = laying
    for side, (count, at, at_r) in zip((above_c, below_c), halo_rows(rows)):
        for i in range(count):
            for c in range(COMP):
                lay_side(a, (c, at + i), side[c * count + i])
            lay_side(n, (at + i,), side[COMP * count + i])
        for i in range(count - 1):
            for c in range(COMP):
                lay_force_side(c, at_r + i, side[(COMP + 1) * count + c * (count - 1) + i])

    first, end, last = BELOW, BELOW + rows, cols // TILE
    coefs([(first - 2, first + 1), (end - 1, end + 3)], rest(last, 1))
    sweep1([(first - 2, first + 1), (end - 1, end + 3)], rest(last, 1))
    sweep2([(first - 1, first + 2), (end - 2, end + 2)], rest(last, 2))
    copies = [
        pltpu.make_async_copy(a.at[c, pl.ds(first, rows), pl.ds(TILE, cols)], smoothed.at[c], sems.at[c])
        for c in range(COMP)
    ]
    for each in copies:
        each.start()
    residual([(first, first + 3), (end - 3, end + 1)], rest(last, 3))

    for c in range(COMP):
        for i in range(rows // 2):
            at = BELOW + 2 * i
            restr[c * (rows // 2) + i] = 0.25 * (b[c, at, TILE:] + b[c, at + 2, TILE:]) + 0.5 * b[c, at + 1, TILE:]
    parts = []
    for i in range(COMP * (rows // 2)):
        p = restr[i, pl.ds(0, cols // 2, stride=2)]
        q = restr[i, pl.ds(1, cols // 2, stride=2)]
        d = restr[i, pl.ds(2, cols // 2, stride=2)]
        parts.append(0.25 * (p + d) + 0.5 * q)
    source = lax.broadcasted_iota(jnp.int32, (lanes, lanes // 2), 0)
    target = 2 * lax.broadcasted_iota(jnp.int32, (lanes, lanes // 2), 1)
    gap = source - target
    h = jnp.where(gap == 1, 0.5, jnp.where((gap == 0) | (gap == 2), 0.25, 0.0))
    for c in range(COMP):
        block = jnp.concatenate(parts[c * (rows // 2) : (c + 1) * (rows // 2)], 0)
        out = jnp.dot(block, h, precision=lax.Precision.HIGHEST, preferred_element_type=jnp.float32)
        coarse[c] = out.reshape(rows // 2, cols // 2, lanes // 2)
    for each in copies:
        each.wait()


def state_shapes(rows, cols, lanes):
    deep, wide = rows + BELOW + ABOVE, cols + TILE
    padded = wide + 2 * TILE
    shapes = (
        (COMP, deep, padded, lanes),
        (COMP, deep, padded, lanes),
        (COMP, deep, wide, lanes),
        (deep, padded, lanes),
        (14, deep, wide, lanes),
        (deep, wide, lanes),
    )
    return [jax.ShapeDtypeStruct(s, jnp.float32) for s in shapes]


def middle(weight, u, rhs, visc):
    vmem = pl.BlockSpec(memory_space=pltpu.VMEM)
    return pl.pallas_call(
        middle_kernel,
        out_shape=state_shapes(*visc.shape),
        in_specs=[vmem] * 4,
        out_specs=[vmem] * 6,
        compiler_params=pltpu.CompilerParams(vmem_limit_bytes=16 << 20),
        cost_estimate=pl.CostEstimate(flops=10_000_000, bytes_accessed=8 << 20, transcendentals=0),
        name="middle",
    )(weight, u, rhs, visc)


def inner(weight, left, right, after, state):
    vmem = pl.BlockSpec(memory_space=pltpu.VMEM)
    return pl.pallas_call(
        inner_kernel,
        out_shape=[jax.ShapeDtypeStruct(x.shape, x.dtype) for x in state],
        in_specs=[vmem] * 3 + [pl.BlockSpec(memory_space=pl.ANY)] + [vmem] * 6,
        out_specs=[vmem] * 6,
        input_output_aliases={4 + i: i for i in range(6)},
        compiler_params=pltpu.CompilerParams(vmem_limit_bytes=16 << 20),
        cost_estimate=pl.CostEstimate(flops=10_000_000, bytes_accessed=8 << 20, transcendentals=0),
        name="inner",
    )(weight, left, right, after, *state)


def outer_middle(weight, above, below, state):
    vmem = pl.BlockSpec(memory_space=pltpu.VMEM)
    return pl.pallas_call(
        outer_middle_kernel,
        out_shape=[jax.ShapeDtypeStruct(x.shape, x.dtype) for x in state],
        in_specs=[vmem] * 9,
        out_specs=[vmem] * 6,
        input_output_aliases={3 + i: i for i in range(6)},
        compiler_params=pltpu.CompilerParams(vmem_limit_bytes=16 << 20),
        cost_estimate=pl.CostEstimate(flops=10_000_000, bytes_accessed=8 << 20, transcendentals=0),
        name="outer_middle",
    )(weight, above, below, *state)


def outer(weight, above_c, below_c, state, rows, cols, lanes):
    vmem = pl.BlockSpec(memory_space=pltpu.VMEM)
    f32 = jnp.float32
    shapes = state_shapes(rows, cols, lanes)
    out = pl.pallas_call(
        outer_kernel,
        out_shape=shapes
        + [
            jax.ShapeDtypeStruct((COMP, rows, cols, lanes), f32),
            jax.ShapeDtypeStruct((COMP, rows // 2, cols // 2, lanes // 2), f32),
        ],
        in_specs=[vmem] * 9,
        out_specs=[vmem] * 6 + [pl.BlockSpec(memory_space=pltpu.HBM), vmem],
        input_output_aliases={3 + i: i for i in range(6)},
        scratch_shapes=[
            pltpu.VMEM((COMP * (rows // 2), cols + 2 * TILE, lanes), f32),
            pltpu.SemaphoreType.DMA((COMP,)),
        ],
        compiler_params=pltpu.CompilerParams(vmem_limit_bytes=16 << 20),
        cost_estimate=pl.CostEstimate(flops=20_000_000, bytes_accessed=16 << 20, transcendentals=0),
        name="outer",
    )(weight, above_c, below_c, *state)
    return out[6], out[7]


def sent(value, axis, steps):
    count = lax.axis_size(axis)
    pairs = [(i, i + steps) for i in range(count) if 0 <= i + steps < count]
    return lax.ppermute(value, axis, pairs)


def per_device(solution, right_side, viscosity, stencil_weights):
    to_left, to_right, to_below, to_above, own_visc, weight = pack(stencil_weights, solution, right_side, viscosity)
    above = sent(to_below, "shell", -1)
    below = sent(to_above, "shell", 1)
    left = sent(to_right, "lat", 1)
    right = sent(to_left, "lat", -1)
    state = middle(weight, solution, right_side, own_visc)
    to_below_c, to_above_c = corners(left, right, state[-1])
    above_c = sent(to_below_c, "shell", -1)
    below_c = sent(to_above_c, "shell", 1)
    state = inner(weight, left, right, to_below_c, state)
    state = outer_middle(weight, above, below, state)
    return outer(weight, above_c, below_c, state, *viscosity.shape)


def solution(mesh):
    in_specs = (
        P(None, "shell", "lat", None),
        P(None, "shell", "lat", None),
        P("shell", "lat", None),
        P(),
    )
    out_specs = (P(None, "shell", "lat", None), P(None, "shell", "lat", None))
    return jax.shard_map(
        per_device, mesh=mesh, in_specs=in_specs, out_specs=out_specs, check_vma=False
    )
```
